32 devices in a mesh: groups: 2 (over y), blk: 8 (over z, x), win: 2 (over core).
Axes of the slice: x: 2, y: 2, z: 4, core: 2. Of those that a mesh axis runs over, the one named last changes fastest.
Arguments:
- spectra: bfloat16 [4, 16, 2, 32, 512], P('win', ('groups', 'blk')), parts along dimension 1, may hold values from -6 to 6
- block_pairs: int32 [32, 2], P('groups'), parts along dimension 0, may hold values from 0 to 7, as said below
- owners: int32 [32, 1], P('groups'), parts along dimension 0, may hold values from 0 to 7; in each aligned block of 16 rows (0 to 15, 16 to 31, ...) at most 3 rows name the same one
- window_mask: int32 [4, 16], P(None, 'groups'), parts along dimension 1, may hold values 0 or 1
Outputs:
- spectra_grad: bfloat16 [4, 16, 2, 32, 512], P('win', ('groups', 'blk')), parts along dimension 1
- slot_misfit: float32 [48], P(('groups', 'blk')), parts along dimension 0
The draws below stay inside these ranges and needn't reach their ends.
There are 2 independent parts, one for each index of `groups`. The reference program is written for one: setup_inputs(seed, part) draws one part's arguments, and reference() takes and returns one part's arrays. A program takes and returns all parts, laid end to end along the dimension named above; each array names one. Nothing has to cross between parts.
Inputs may be any that keep to these rules, and one draw needn't show every extreme that they name: `block_pairs`: each row names two blocks, the first smaller than the second; a pair may be listed more than once. `owners`: no index of blk owns more than 3 pairs, and some index owns exactly 3; every index owns at least one.
All inputs are finite; a program needn't handle non-finite values.
Results may differ from the reference program's by a relative error of at most 0.0047.
Values may be sent and summed in bfloat16 or wider, within the bound.
No kernel may reach another device: no remote copies, remote signals or barrier semaphores. Data moves between devices by JAX's collectives and lax.ppermute only.
A program may use at most 128 MiB of HBM per device.

```python
import math
import jax
import jax.numpy as jnp
import numpy as np
from jax import lax

CHAN = 32
FREQ = 512
WINDOWS = 4
CAP = 3
BLOCKS = 8
PAIRS = 16
LAGS = 1024
N_BLK = 8


def draw_block_pairs(key, part):
    key_first, key_second = jax.random.split(jax.random.fold_in(key, 11))
    first_ids = jax.random.randint(key_first, (PAIRS,), 0, BLOCKS - 1)
    second_ids = jax.random.randint(key_second, (PAIRS,), first_ids + 1, BLOCKS)
    row_index = jnp.arange(PAIRS)
    first_ids = jnp.where(row_index == 0, 0, first_ids)
    second_ids = jnp.where(row_index == 0, BLOCKS - 1, second_ids)
    return jnp.stack([first_ids, second_ids], axis=1).astype(jnp.int32)


def place_ends(entries, key, low, high):
    longest = entries.shape.index(max(entries.shape))
    spots = []
    for shift in (0, 1):
        where = [jax.random.randint(jax.random.fold_in(key, axis), (), 0, length) for axis, length in enumerate(entries.shape)]
        where[longest] = (where[longest] + shift) % entries.shape[longest]
        spots.append(tuple(where))
    return entries.at[spots[0]].set(low).at[spots[1]].set(high)


def levels(own_key, dims, cuts, smallest, high):
    level, own = 1.0, jax.random.fold_in(own_key, 6)
    for dim, shards_of in cuts:
        heights = jnp.exp(jax.random.uniform(jax.random.fold_in(own, dim), (shards_of,), jnp.float32, smallest / len(cuts), high / len(cuts)))
        level = level * jnp.repeat(heights, dims[dim] // shards_of).reshape([-1 if axis == dim else 1 for axis in range(len(dims))])
    return level


def assign_block(key, own, number, rows, count, top, reach, lean):
    sequence = jax.random.permutation(key, count)
    packed, usual = shares(count, rows * top, reach, lean, True), shares(count, rows * top, reach, lean, False)
    places = jnp.arange(count)

    def named(sizes, offset_by):
        used = int((sizes > 0).sum())
        fixed = max(1, used // 4)
        shifted = fixed + (places - fixed + offset_by * (used - fixed)) % max(1, count - fixed)
        return jnp.zeros((count,), jnp.int32).at[sequence[jnp.where(places < fixed, places, shifted)]].set(jnp.asarray(sizes, jnp.int32))

    sizes = jnp.where(number % 4 == 0, named(packed, number // 4), named(usual, number - number // 4 - 1))
    mixed = jax.random.permutation(jax.random.fold_in(own, 3), count)
    donor, taker = mixed[0:count // 2 * 2:2], mixed[1:count // 2 * 2:2]
    slack = jnp.minimum(sizes[donor] - 1, reach - sizes[taker]) // 2
    slack = jnp.where((donor == sequence[0]) | (taker == sequence[0]) | (sizes[taker] == 0), 0, jnp.maximum(slack, 0))
    shifted = jax.random.randint(jax.random.fold_in(own, 4), (count // 2,), 0, 1 << 20) % (slack + 1)
    sizes = sizes.at[donor].add(-shifted).at[taker].add(shifted)
    members = jnp.searchsorted(jnp.cumsum(sizes), jnp.arange(rows * top), side="right").astype(jnp.int32)
    grid = members.reshape(top, rows).T
    grid = grid[jax.random.permutation(jax.random.fold_in(own, 1), rows)]
    offset_by = jax.random.randint(jax.random.fold_in(own, 2), (rows, 1), 0, top)
    return jnp.take_along_axis(grid, (jnp.arange(top)[None, :] + offset_by) % top, axis=1)


def shares(number_of, total, limit, skew, full):
    portions = [(1 << 20) // math.isqrt(rank ** skew) + 1 for rank in range(1, number_of + 1)]
    largest = limit if full else min(limit, max(-(-total // number_of), total * portions[0] // sum(portions)))
    least = 1 if total - largest >= number_of - 1 else 0
    counts, rest = [largest] + [least] * (number_of - 1), total - largest - least * (number_of - 1)
    while rest > 0:
        movable = [i for i in range(1, number_of) if counts[i] < largest] or [i for i in range(1, number_of) if counts[i] < limit]
        whole, left = sum([portions[i] for i in movable]), rest
        for i in movable:
            more = min(limit - counts[i], max(1, left * portions[i] // whole), rest)
            counts[i] = counts[i] + more
            rest = rest - more
    return np.array(counts)


def scatter_about(stream_key, dims, spread, bound, cuts=(), kind=jnp.bfloat16):
    entries = spread * jax.random.normal(stream_key, dims, jnp.float32)
    if cuts:
        entries = entries * levels(stream_key, dims, cuts, -0.22, 0.18)
    return jnp.clip(entries, -bound, bound).astype(kind)


def setup_inputs(seed: int = 0, part: int = 0) -> dict:
    key_list = jax.random.split(jax.random.key(seed), 5)
    own_keys = jax.random.split(jax.random.fold_in(key_list[4], part), 5)
    spectra = scatter_about(own_keys[0], (WINDOWS, BLOCKS, 2, CHAN, FREQ), 1.0, 6.0, ((0, 2), (1, 8)))
    block_pairs = draw_block_pairs(jax.random.fold_in(jax.random.fold_in(key_list[4], part), 71), part)
    owners_keys = jax.random.split(jax.random.fold_in(own_keys[2], 1), PAIRS // PAIRS)
    owners_turns = jax.random.permutation(jax.random.fold_in(own_keys[2], 3), PAIRS // PAIRS)
    owners = jax.vmap(lambda own, number: assign_block(jax.random.fold_in(own_keys[2], 2), own, number, PAIRS, N_BLK, 1, CAP, 2))(owners_keys, owners_turns).reshape((PAIRS, 1))
    window_mask = place_ends((jax.random.randint(own_keys[3], (WINDOWS, BLOCKS), 0, 4) < 3).astype(jnp.int32), jax.random.fold_in(own_keys[3], 1), 0, 1)
    return {"spectra": spectra, "block_pairs": block_pairs, "owners": owners, "window_mask": window_mask}


def dft_tables(freq_count, lag_count):
    f_index = jnp.arange(freq_count, dtype=jnp.int32)[:, None]
    t_index = jnp.arange(lag_count, dtype=jnp.int32)[None, :]
    phase = (f_index * t_index % lag_count).astype(jnp.float32) * (2.0 * math.pi / lag_count)
    return jnp.stack([jnp.cos(phase).astype(jnp.bfloat16), (-jnp.sin(phase)).astype(jnp.bfloat16)])

def lag_weight(lag_count):
    return 1.0 + jnp.cos(jnp.arange(lag_count, dtype=jnp.float32) * (math.pi / lag_count))

def slot_tables(owner_ids, owners_total, capacity):
    pair_count = owner_ids.shape[0]
    onehot = (owner_ids[:, None] == jnp.arange(owners_total, dtype=jnp.int32)[None, :]).astype(jnp.int32)
    earlier = (jnp.cumsum(onehot, axis=0) - onehot).astype(jnp.int32)
    rank_in = lax.optimization_barrier(jnp.sum(earlier * onehot, axis=1)).astype(jnp.int32)
    slot_of_pair = (owner_ids * capacity + rank_in).astype(jnp.int32)
    slots_total = owners_total * capacity
    matches = (slot_of_pair[None, :] == jnp.arange(slots_total, dtype=jnp.int32)[:, None]).astype(jnp.int32)
    numbers = jnp.arange(pair_count, dtype=jnp.int32)[None, :] + 1
    pair_of_slot = (lax.optimization_barrier(jnp.sum(matches * numbers, axis=1)) - 1).astype(jnp.int32)
    return (slot_of_pair, pair_of_slot)

def reference(spectra, block_pairs, owners, window_mask):
    highest = lax.Precision.HIGHEST
    tables = dft_tables(FREQ, LAGS).astype(jnp.float32)
    lag_taper = lag_weight(LAGS)
    mask_f = window_mask.astype(jnp.float32)

    def toward_second(adjoint_part, spectrum):
        return jnp.einsum('xyf,wxf->wyf', adjoint_part, spectrum, precision=highest)

    def toward_first(adjoint_part, spectrum):
        return jnp.einsum('xyf,wyf->wxf', adjoint_part, spectrum, precision=highest)

    def one_pair(gradient, pair_index):
        first_id = block_pairs[pair_index, 0]
        second_id = block_pairs[pair_index, 1]
        left_spec = lax.dynamic_index_in_dim(spectra, first_id, 1, keepdims=False).astype(jnp.float32)
        right_spec = lax.dynamic_index_in_dim(spectra, second_id, 1, keepdims=False).astype(jnp.float32)
        pair_weight = mask_f[:, first_id] * mask_f[:, second_id]
        a_left = left_spec[:, 0]
        b_left = left_spec[:, 1]
        a_right = right_spec[:, 0]
        b_right = right_spec[:, 1]
        real_sum = jnp.zeros((CHAN, CHAN, FREQ), jnp.float32)
        imag_sum = jnp.zeros((CHAN, CHAN, FREQ), jnp.float32)
        for window in range(WINDOWS):
            w_here = pair_weight[window]
            real_sum = real_sum + w_here * (a_left[window][:, None, :] * a_right[window][None, :, :] + b_left[window][:, None, :] * b_right[window][None, :, :])
            imag_sum = imag_sum + w_here * (a_left[window][:, None, :] * b_right[window][None, :, :] - b_left[window][:, None, :] * a_right[window][None, :, :])
        cross_spec = lax.optimization_barrier(jnp.stack([real_sum, imag_sum]).astype(jnp.bfloat16)).astype(jnp.float32)
        shared = jnp.sum(pair_weight)
        denom = jnp.sqrt(2.0 * FREQ * jnp.maximum(shared, 1.0))
        lagged = lax.dot_general(cross_spec.reshape(2, CHAN * CHAN, FREQ), tables, (((0, 2), (0, 1)), ((), ())), precision=highest) / denom
        mirror = jnp.roll(jnp.flip(lagged, axis=1), 1, axis=1)
        residual = lagged - 0.5 * mirror
        adj_source = (lag_taper * residual * residual * residual / 8.0).astype(jnp.bfloat16)
        squared = residual * residual
        misfit = jnp.sum(lag_taper * squared * squared) / (8.0 * CHAN * CHAN * LAGS)
        adj_wide = lax.optimization_barrier(adj_source).astype(jnp.float32)
        adjoint = jnp.einsum('kt,rft->rkf', adj_wide, tables, precision=highest) / (denom * math.sqrt(CHAN))
        adjoint = lax.optimization_barrier(adjoint.astype(jnp.bfloat16)).astype(jnp.float32).reshape(2, CHAN, CHAN, FREQ)
        g_real = adjoint[0]
        g_imag = adjoint[1]
        d_a_right = toward_second(g_real, a_left) - toward_second(g_imag, b_left)
        d_b_right = toward_second(g_real, b_left) + toward_second(g_imag, a_left)
        d_a_left = toward_first(g_real, a_right) + toward_first(g_imag, b_right)
        d_b_left = toward_first(g_real, b_right) - toward_first(g_imag, a_right)
        weight_col = pair_weight[:, None, None, None]
        first_term = jnp.stack([d_a_left, d_b_left], axis=1) * weight_col
        second_term = jnp.stack([d_a_right, d_b_right], axis=1) * weight_col
        gradient = gradient.at[:, first_id].add(first_term)
        gradient = gradient.at[:, second_id].add(second_term)
        return (gradient, misfit)
    start = jnp.zeros((WINDOWS, BLOCKS, 2, CHAN, FREQ), jnp.float32)
    gradient, misfits = lax.scan(one_pair, start, jnp.arange(PAIRS, dtype=jnp.int32))
    slot_of_pair, pair_of_slot = slot_tables(owners[:, 0], N_BLK, CAP)
    slot_misfit = jnp.where(pair_of_slot >= 0, misfits[jnp.maximum(pair_of_slot, 0)], jnp.zeros((), misfits.dtype))
    return (gradient.astype(jnp.bfloat16), slot_misfit)
```

```python
import functools
import math

import jax
import jax.numpy as jnp
import ml_dtypes
import numpy as np
from jax import lax
from jax.experimental import pallas as pl
from jax.experimental.pallas import tpu as pltpu
from jax.sharding import PartitionSpec as P

CAP = 3
PARTS = 4
TEAM = 8
SUBSETS = ((0, 1), (0, 1), (0, 2), (0, 3), (1, 2), (1, 3), (2, 3), (2, 3))
GROUP = 4


@functools.lru_cache(maxsize=None)
def tables(freq_count):
    lag_count = 2 * freq_count
    f = np.arange(freq_count)[:, None]
    t = np.arange(freq_count)[None, :]
    phase = (f * t % lag_count) * (2.0 * np.pi / lag_count)
    cos = np.cos(phase)
    sin = -np.sin(phase)
    alternate = np.where(np.arange(freq_count) % 2 == 0, 1.0, -1.0)
    extra = np.zeros((freq_count, 128))
    extra[:, 0] = alternate
    forward_re = np.concatenate([cos, extra], axis=1)
    cos_back = cos.T
    cos_mirror = cos_back.copy()
    cos_mirror[0] = alternate
    back_re = np.concatenate([cos_back, cos_mirror], axis=0)
    back_im = np.concatenate([sin.T, -sin.T], axis=0)
    taper = 1.0 + np.cos(np.pi * np.arange(lag_count) / lag_count)
    mirror = np.concatenate([[freq_count], lag_count - np.arange(1, freq_count)])
    weight = np.stack([taper[:freq_count], taper[mirror]]) / 8.0
    as_bf16 = lambda x: x.astype(np.float32).astype(ml_dtypes.bfloat16)
    return (
        as_bf16(forward_re),
        as_bf16(sin),
        as_bf16(back_re),
        as_bf16(back_im),
        weight.astype(np.float32),
    )


def pair_kernel(
    meta,
    pairs,
    mask,
    own,
    other,
    forward_re,
    forward_im,
    back_re,
    back_im,
    weight,
    own_grad,
    other_grad,
    misfit,
    first,
    second,
    cross_re,
    cross_im,
    adj,
    out_re,
    out_im,
):
    pair_count = misfit.shape[0]
    freq = own.shape[-1]
    part = own.shape[3] // 2
    local = own.shape[1]
    base = meta[0]
    first_part = meta[1] * part
    second_part = meta[2] * part
    core = meta[3]
    rows = part * part
    lanes = 256

    own_grad[...] = jnp.zeros_like(own_grad)
    other_grad[...] = jnp.zeros_like(other_grad)

    def work(step, carry):
        counts = []
        for k in range(GROUP):
            p = step * GROUP + k
            i = pairs[base + p, 0]
            j = pairs[base + p, 1]
            shared = jnp.int32(0)
            for w in range(2 * local):
                is_own = w < local
                source = own if is_own else other
                side = core if is_own else 1 - core
                where = side * local + w % local
                m = mask[where, i] * mask[where, j]
                shared = shared + m
                m = m.astype(jnp.float32)
                for c in range(2):
                    at = k * 4 * local + w * 2 + c
                    first[at] = source[i, w % local, c, pl.ds(first_part, part)].astype(jnp.float32) * m
                    second[at] = source[j, w % local, c, pl.ds(second_part, part)].astype(jnp.float32) * m
            counts.append(jnp.maximum(shared, 1).astype(jnp.float32) * (2.0 * freq))
            for chunk in range(freq // lanes):
                cut = pl.ds(chunk * lanes, lanes)
                right = [second[k * 4 * local + n, :, cut] for n in range(4 * local)]
                for c1 in range(part):
                    re = None
                    for w in range(2 * local):
                        a = first[k * 4 * local + 2 * w, pl.ds(c1, 1), cut]
                        b = first[k * 4 * local + 2 * w + 1, pl.ds(c1, 1), cut]
                        aa = a * right[2 * w] + b * right[2 * w + 1]
                        ab = a * right[2 * w + 1] - b * right[2 * w]
                        re = aa if re is None else re + aa
                        im = ab if w == 0 else im + ab
                    cross_re[pl.ds(k * rows + c1 * part, part), cut] = re.astype(jnp.bfloat16)
                    cross_im[pl.ds(k * rows + c1 * part, part), cut] = im.astype(jnp.bfloat16)

        cos_sum = jnp.dot(cross_re[...], forward_re[...], preferred_element_type=jnp.float32)
        sin_sum = jnp.dot(cross_im[...], forward_im[...], preferred_element_type=jnp.float32)
        lane = lax.broadcasted_iota(jnp.int32, (rows, freq), 1)
        for k in range(GROUP):
            cut = slice(k * rows, (k + 1) * rows)
            scale = 0.5 * lax.rsqrt(jnp.full((1, freq), counts[k], jnp.float32))
            even = cos_sum[cut, :freq] * scale
            odd = sin_sum[cut] * (3.0 * scale)
            middle = cos_sum[cut, freq : freq + 1] * scale
            plus = even + odd
            minus = jnp.where(lane == 0, middle, even - odd)
            plus_adj = plus * plus * plus * weight[0:1, :]
            minus_adj = minus * minus * minus * weight[1:2, :]
            adj[cut, :freq] = plus_adj.astype(jnp.bfloat16)
            adj[cut, freq:] = minus_adj.astype(jnp.bfloat16)
            total = plus_adj * plus + minus_adj * minus
            misfit[pl.ds(step * GROUP + k, 1), :] = jnp.sum(total, axis=0, keepdims=True)
        g_sum = jnp.dot(adj[...], back_re[...], preferred_element_type=jnp.float32)
        h_sum = jnp.dot(adj[...], back_im[...], preferred_element_type=jnp.float32)
        for k in range(GROUP):
            cut = slice(k * rows, (k + 1) * rows)
            scale = lax.rsqrt(jnp.full((1, freq), counts[k] * (4.0 * part), jnp.float32))
            g_out = (g_sum[cut] * scale).astype(jnp.bfloat16).astype(jnp.float32)
            h_out = (h_sum[cut] * scale).astype(jnp.bfloat16).astype(jnp.float32)
            for chunk in range(freq // 128):
                out_re[chunk, cut] = g_out[:, chunk * 128 : (chunk + 1) * 128]
                out_im[chunk, cut] = h_out[:, chunk * 128 : (chunk + 1) * 128]

        for k in range(GROUP):
            p = step * GROUP + k
            i = pairs[base + p, 0]
            j = pairs[base + p, 1]
            at = k * 4 * local
            for chunk in range(freq // 128):
                cut = pl.ds(chunk * 128, 128)
                to_second = [None] * (4 * local)
                to_first = [None] * (4 * local)
                add = lambda total, term: term if total is None else total + term
                for c in range(part):
                    g = out_re[chunk, pl.ds(k * rows + c * part, part)]
                    h = out_im[chunk, pl.ds(k * rows + c * part, part)]
                    for w in range(2 * local):
                        a = first[at + 2 * w, pl.ds(c, 1), cut]
                        b = first[at + 2 * w + 1, pl.ds(c, 1), cut]
                        to_second[2 * w] = add(to_second[2 * w], g * a - h * b)
                        to_second[2 * w + 1] = add(to_second[2 * w + 1], g * b + h * a)
                for w in range(2 * local):
                    target = own_grad if w < local else other_grad
                    for c in range(2):
                        target[j, w % local, c, pl.ds(second_part, part), cut] += to_second[2 * w + c]
                for c in range(part):
                    g = out_re[chunk, pl.ds(k * rows + c, part, stride=part)]
                    h = out_im[chunk, pl.ds(k * rows + c, part, stride=part)]
                    for w in range(2 * local):
                        a = second[at + 2 * w, pl.ds(c, 1), cut]
                        b = second[at + 2 * w + 1, pl.ds(c, 1), cut]
                        to_first[2 * w] = add(to_first[2 * w], g * a + h * b)
                        to_first[2 * w + 1] = add(to_first[2 * w + 1], g * b - h * a)
                for w in range(2 * local):
                    target = own_grad if w < local else other_grad
                    for c in range(2):
                        target[i, w % local, c, pl.ds(first_part, part), cut] += to_first[2 * w + c]
        return carry

    lax.fori_loop(0, pair_count // GROUP, work, 0)


def per_device(spectra, block_pairs, owners, window_mask):
    blk_count = lax.axis_size("blk")
    win_count = lax.axis_size("win")
    blk_index = lax.axis_index("blk")
    core = lax.axis_index("win")
    local = spectra.shape[0]
    channels = spectra.shape[3]
    freq = spectra.shape[4]
    part = channels // PARTS
    pair_total = block_pairs.shape[0]
    teams = blk_count // TEAM
    pair_count = pair_total // teams
    rank = blk_index % TEAM
    team = blk_index // TEAM

    pieces = spectra[:, 0].reshape(local, 2, PARTS, part, freq)
    outgoing = jnp.stack(
        [jnp.stack([pieces[:, :, s] for s in SUBSETS[r]], axis=2) for r in range(TEAM)]
    ).reshape(TEAM, local, 2, 2 * part, freq)
    outgoing = jnp.tile(outgoing, (teams, 1, 1, 1, 1))
    own = lax.all_to_all(outgoing, "blk", split_axis=0, concat_axis=0, tiled=True)
    swap = [(0, 1), (1, 0)]
    other = lax.ppermute(own, "win", swap)

    same = (rank == 0) | (rank == TEAM - 1)
    meta = jnp.stack(
        [team * pair_count, core, jnp.where(same, core, 1 - core), core]
    ).astype(jnp.int32)
    forward_re, forward_im, back_re, back_im, weight = tables(freq)
    smem = pl.BlockSpec(memory_space=pltpu.SMEM)
    vmem = pl.BlockSpec(memory_space=pltpu.VMEM)
    grad_type = jax.ShapeDtypeStruct((blk_count, local, 2, 2 * part, freq), jnp.float32)
    rows = part * part * GROUP
    grad_bytes = math.prod(grad_type.shape) * 4
    own_grad, other_grad, misfit = pl.pallas_call(
        pair_kernel,
        out_shape=(grad_type, grad_type, jax.ShapeDtypeStruct((pair_count, freq), jnp.float32)),
        in_specs=[smem] * 3 + [vmem] * 7,
        out_specs=(vmem, vmem, vmem),
        scratch_shapes=[
            pltpu.VMEM((GROUP * 4 * local, part, freq), jnp.float32),
            pltpu.VMEM((GROUP * 4 * local, part, freq), jnp.float32),
            pltpu.VMEM((rows, freq), jnp.bfloat16),
            pltpu.VMEM((rows, freq), jnp.bfloat16),
            pltpu.VMEM((rows, 2 * freq), jnp.bfloat16),
            pltpu.VMEM((freq // 128, rows, 128), jnp.float32),
            pltpu.VMEM((freq // 128, rows, 128), jnp.float32),
        ],
        compiler_params=pltpu.CompilerParams(vmem_limit_bytes=(16 << 20) + 3 * grad_bytes),
    )(
        meta,
        block_pairs,
        window_mask,
        own,
        other,
        forward_re,
        forward_im,
        back_re,
        back_im,
        weight,
    )

    came = lax.ppermute(other_grad.astype(jnp.bfloat16), "win", swap)
    terms = jnp.sum(misfit, axis=1)
    terms = terms + lax.ppermute(terms, "win", swap)
    chip_grad = (own_grad + came.astype(jnp.float32)).astype(jnp.bfloat16)
    high = terms.astype(jnp.bfloat16)
    low = (terms - high.astype(jnp.float32)).astype(jnp.bfloat16)
    note = jnp.zeros((8, freq), jnp.bfloat16).at[0, :pair_count].set(high).at[1, :pair_count].set(low)
    grad_rows = local * 2 * 2 * part
    payload = jnp.concatenate(
        [
            chip_grad.reshape(blk_count, grad_rows, freq),
            jnp.broadcast_to(note[None], (blk_count, 8, freq)),
        ],
        axis=1,
    )
    arrived = lax.all_to_all(payload, "blk", split_axis=0, concat_axis=0, tiled=True)
    wide = arrived[:, :grad_rows].reshape(teams, TEAM, local, 2, 2, part, freq).astype(jnp.float32)
    wide = jnp.sum(wide, axis=0)
    gradient = jnp.stack(
        [
            sum(wide[r, :, :, SUBSETS[r].index(s)] for r in range(TEAM) if s in SUBSETS[r])
            for s in range(PARTS)
        ],
        axis=2,
    )
    gradient = gradient.reshape(local, 1, 2, channels, freq).astype(jnp.bfloat16)
    notes = arrived[:, grad_rows:, :pair_count].astype(jnp.float32)
    notes = jnp.sum((notes[:, 0] + notes[:, 1]).reshape(teams, TEAM, pair_count), axis=1)
    pair_misfit = notes.reshape(pair_total) / (channels * channels * 2.0 * freq)

    owner_ids = owners[:, 0]
    order = jnp.arange(pair_total, dtype=jnp.int32)
    earlier = (owner_ids[:, None] == owner_ids[None, :]) & (order[None, :] < order[:, None])
    slot = owner_ids * CAP + jnp.sum(earlier.astype(jnp.int32), axis=1)
    mine = blk_index * CAP + jnp.arange(CAP, dtype=jnp.int32)
    totals = jnp.sum(jnp.where(slot[None, :] == mine[:, None], pair_misfit[None, :], 0.0), axis=1)
    return (gradient, totals)


def solution(mesh):
    return jax.shard_map(
        per_device,
        mesh=mesh,
        in_specs=(
            P("win", ("groups", "blk"), None, None, None),
            P("groups", None),
            P("groups", None),
            P(None, "groups"),
        ),
        out_specs=(P("win", ("groups", "blk"), None, None, None), P(("groups", "blk"))),
        check_vma=False,
    )
```

```python
import functools
import math

import jax
import jax.numpy as jnp
import ml_dtypes
import numpy as np
from jax import lax
from jax.experimental import pallas as pl
from jax.experimental.pallas import tpu as pltpu
from jax.sharding import PartitionSpec as P

CAP = 3
PARTS = 4
TEAM = 8
SUBSETS = ((0, 1), (0, 1), (0, 2), (0, 3), (1, 2), (1, 3), (2, 3), (2, 3))
GROUP = 4
HOPS = ((6, 4, 2, 0), (7, 5, 3, 1))


@functools.lru_cache(maxsize=None)
def tables(freq_count):
    lag_count = 2 * freq_count
    f = np.arange(freq_count)[:, None]
    t = np.arange(freq_count)[None, :]
    phase = (f * t % lag_count) * (2.0 * np.pi / lag_count)
    cos = np.cos(phase)
    sin = -np.sin(phase)
    alternate = np.where(np.arange(freq_count) % 2 == 0, 1.0, -1.0)
    extra = np.zeros((freq_count, 128))
    extra[:, 0] = alternate
    forward_re = np.concatenate([cos, extra], axis=1)
    cos_back = cos.T
    cos_mirror = cos_back.copy()
    cos_mirror[0] = alternate
    back_re = np.concatenate([cos_back, cos_mirror], axis=0)
    back_im = np.concatenate([sin.T, -sin.T], axis=0)
    taper = 1.0 + np.cos(np.pi * np.arange(lag_count) / lag_count)
    mirror = np.concatenate([[freq_count], lag_count - np.arange(1, freq_count)])
    weight = np.stack([taper[:freq_count], taper[mirror]]) / 8.0
    as_bf16 = lambda x: x.astype(np.float32).astype(ml_dtypes.bfloat16)
    return (
        as_bf16(forward_re),
        as_bf16(sin),
        as_bf16(back_re),
        as_bf16(back_im),
        weight.astype(np.float32),
    )


@functools.lru_cache(maxsize=None)
def positions():
    out = np.zeros((TEAM, 2, 20), np.int32)
    for rank in range(TEAM):
        for core in range(2):
            same = rank in (0, TEAM - 1)
            row = [0, core, core if same else 1 - core, core]
            row += [rank ^ hop for hop in HOPS[core]]
            row += [rank ^ hop for hop in HOPS[1 - core]]
            for hop in HOPS[core]:
                row += SUBSETS[rank ^ hop]
            out[rank, core] = row
    return out


def pack_kernel(meta, own, other, *refs):
    parcels, wide = refs[:-1], refs[-1]
    local = own.shape[0]
    core = meta[3]
    for source, side in ((own, core), (other, 1 - core)):
        for w in range(local):
            for c in range(2):
                wide[...] = source[w, 0, c].astype(jnp.float32).reshape(wide.shape)
                for r, parcel in enumerate(parcels):
                    both = [wide[meta[12 + 2 * r + n]] for n in range(2)]
                    parcel[side * local + w, c] = jnp.concatenate(both, axis=0).astype(jnp.bfloat16)


def add_kernel(keep, came, terms, *parcels):
    count = len(parcels)
    rows = keep.shape[0] // count
    pair_count = terms.shape[0]
    half = pair_count // 2
    arrived = came[count * rows :].astype(jnp.float32)
    total = terms[...] + jnp.concatenate(
        [arrived[:, :128] + arrived[:, 256:384], arrived[:, 128:256] + arrived[:, 384:512]], axis=0
    )
    note = note_of(total, half)
    for r, parcel in enumerate(parcels):
        cut = slice(r * rows, (r + 1) * rows)
        parcel[:rows] = (keep[cut] + came[cut].astype(jnp.float32)).astype(jnp.bfloat16)
        parcel[rows:] = note


def note_of(total, half):
    high = total.astype(jnp.bfloat16).astype(jnp.float32)
    low = total - high
    return jnp.concatenate([high[:half], high[half:], low[:half], low[half:]], axis=1).astype(
        jnp.bfloat16
    )


def merge_kernel(meta, *refs):
    parcels, (mine, give, total) = refs[: len(HOPS[0])], refs[len(HOPS[0]) :]
    windows, _, _, part, freq = total.shape
    channels = PARTS * part
    local = windows // 2
    core = meta[3]
    rows = windows * 2 * 2 * part
    note = None
    total[...] = jnp.zeros_like(total)
    for r, parcel in enumerate(parcels):
        for w in range(windows):
            for c in range(2):
                for n in range(2):
                    start = ((w * 2 + c) * 2 + n) * part
                    term = parcel[start : start + part].astype(jnp.float32)
                    total[w, c, meta[12 + 2 * r + n]] += term
        tail = parcel[rows:].astype(jnp.float32)
        tail = jnp.concatenate(
            [tail[:, :128] + tail[:, 256:384], tail[:, 128:256] + tail[:, 384:512]], axis=0
        )
        note = tail if note is None else note + tail
    for w in range(local):
        for c in range(2):
            to = slice((w * 2 + c) * channels, (w * 2 + c + 1) * channels)
            mine[to] = total[core * local + w, c].reshape(channels, freq)
            give[to] = total[(1 - core) * local + w, c].reshape(channels, freq)
    body = local * 2 * channels
    pad = jnp.zeros((note.shape[0], freq - 128), jnp.float32)
    mine[body:] = jnp.concatenate([note, pad], axis=1)
    give[body:] = jnp.concatenate([note, pad], axis=1)


def finish_kernel(mine, came, chosen, gradient, totals, scale):
    local, _, _, channels, _ = gradient.shape
    for w in range(local):
        for c in range(2):
            cut = slice((w * 2 + c) * channels, (w * 2 + c + 1) * channels)
            gradient[w, 0, c] = (mine[cut] + came[cut]).astype(jnp.bfloat16)
    body = local * 2 * channels
    note = mine[body:, :128] + came[body:, :128]
    pair = jnp.sum(note, axis=1, keepdims=True) * scale
    totals[...] = jnp.sum(pair * chosen[...], axis=0, keepdims=True)


def pair_kernel(
    direct,
    pair_count,
    meta,
    pairs,
    mask,
    *refs,
):
    sources = 2 * len(HOPS[0]) if direct else 2
    came, refs = refs[:sources], refs[sources:]
    (
        forward_re_hbm,
        forward_im_hbm,
        back_re_hbm,
        back_im_hbm,
        weight,
        own_grad,
        other_grad,
        misfit,
        first,
        second,
        cross_re,
        cross_im,
        adj,
        out_re,
        out_im,
        forward_re,
        forward_im,
        back_re,
        back_im,
        sems,
    ) = refs[:20]
    copies = [
        pltpu.make_async_copy(source, target, sems.at[n])
        for n, (source, target) in enumerate(
            (
                (forward_re_hbm, forward_re),
                (forward_im_hbm, forward_im),
                (back_re_hbm, back_re),
                (back_im_hbm, back_im),
            )
        )
    ]
    for copy in copies:
        copy.start()
    freq = came[0].shape[-1]
    part = came[0].shape[-2] // 2
    local = mask.shape[0] // 2
    base = meta[0]
    first_part = meta[1]
    second_part = meta[2]
    core = meta[3]
    rows = part * part
    lanes = 256

    if direct:
        field, grad = refs[20:]
        for n, parcel in enumerate(came):
            index = meta[4 + n]
            for w in range(2 * local):
                m = mask[w, index].astype(jnp.float32)
                for c in range(2):
                    field[index, w, c] = (parcel[w, c].astype(jnp.float32) * m).reshape(2, part, freq)
        grad[...] = jnp.zeros_like(grad)
    else:
        own_grad[...] = jnp.zeros_like(own_grad)
        other_grad[...] = jnp.zeros_like(other_grad)

    def block(index, w, c, which):
        both = came[w // local][index, w % local, c].astype(jnp.float32)
        return jnp.where(which == 0, both[:part], both[part:])

    def first_row(k, i, w, c, row, cut):
        if direct:
            return field[i, w, c, first_part, pl.ds(row, 1), cut]
        return first[(k * 2 * local + w) * 2 + c, pl.ds(row, 1), cut]

    def second_row(k, j, w, c, row, cut):
        if direct:
            return field[j, w, c, second_part, pl.ds(row, 1), cut]
        return second[(k * 2 * local + w) * 2 + c, pl.ds(row, 1), cut]

    def add_to(index, w, c, which, cut, term):
        if direct:
            grad[index, w, c, which, :, cut] += term
        else:
            target = own_grad if w < local else other_grad
            target[index, w % local, c, pl.ds(which * part, part), cut] += term

    def work(step, carry):
        counts = []
        for k in range(GROUP):
            p = step * GROUP + k
            i = pairs[base + p, 0]
            j = pairs[base + p, 1]
            shared = jnp.int32(0)
            for w in range(2 * local):
                side = core if w < local else 1 - core
                where = w if direct else side * local + w % local
                m = mask[where, i] * mask[where, j]
                shared = shared + m
                if direct:
                    continue
                m = m.astype(jnp.float32)
                for c in range(2):
                    at = k * 4 * local + w * 2 + c
                    first[at] = block(i, w, c, first_part) * m
                    second[at] = block(j, w, c, second_part) * m
            counts.append(jnp.maximum(shared, 1).astype(jnp.float32) * (2.0 * freq))
            for chunk in range(freq // lanes):
                cut = pl.ds(chunk * lanes, lanes)
                if direct:
                    right = [field[j, n // 2, n % 2, second_part, :, cut] for n in range(4 * local)]
                else:
                    right = [second[k * 4 * local + n, :, cut] for n in range(4 * local)]
                for c1 in range(part):
                    re = None
                    for w in range(2 * local):
                        a = first_row(k, i, w, 0, c1, cut)
                        b = first_row(k, i, w, 1, c1, cut)
                        aa = a * right[2 * w] + b * right[2 * w + 1]
                        ab = a * right[2 * w + 1] - b * right[2 * w]
                        re = aa if re is None else re + aa
                        im = ab if w == 0 else im + ab
                    cross_re[pl.ds(k * rows + c1 * part, part), cut] = re.astype(jnp.bfloat16)
                    cross_im[pl.ds(k * rows + c1 * part, part), cut] = im.astype(jnp.bfloat16)

        @pl.when(step == 0)
        def _():
            for copy in copies:
                copy.wait()

        cos_sum = jnp.dot(cross_re[...], forward_re[...], preferred_element_type=jnp.float32)
        sin_sum = jnp.dot(cross_im[...], forward_im[...], preferred_element_type=jnp.float32)
        lane = lax.broadcasted_iota(jnp.int32, (rows, freq), 1)
        for k in range(GROUP):
            cut = slice(k * rows, (k + 1) * rows)
            scale = 0.5 * lax.rsqrt(jnp.full((1, freq), counts[k], jnp.float32))
            even = cos_sum[cut, :freq] * scale
            odd = sin_sum[cut] * (3.0 * scale)
            middle = cos_sum[cut, freq : freq + 1] * scale
            plus = even + odd
            minus = jnp.where(lane == 0, middle, even - odd)
            plus_adj = plus * plus * plus * weight[0:1, :]
            minus_adj = minus * minus * minus * weight[1:2, :]
            adj[cut, :freq] = plus_adj.astype(jnp.bfloat16)
            adj[cut, freq:] = minus_adj.astype(jnp.bfloat16)
            total = plus_adj * plus + minus_adj * minus
            total = jnp.sum(total, axis=0, keepdims=True)
            total = sum(total[:, n : n + 128] for n in range(0, freq, 128))
            misfit[pl.ds(step * GROUP + k, 1), :] = total
        g_sum = jnp.dot(adj[...], back_re[...], preferred_element_type=jnp.float32)
        h_sum = jnp.dot(adj[...], back_im[...], preferred_element_type=jnp.float32)
        for k in range(GROUP):
            cut = slice(k * rows, (k + 1) * rows)
            scale = lax.rsqrt(jnp.full((1, freq), counts[k] * (4.0 * part), jnp.float32))
            g_out = (g_sum[cut] * scale).astype(jnp.bfloat16).astype(jnp.float32)
            h_out = (h_sum[cut] * scale).astype(jnp.bfloat16).astype(jnp.float32)
            for chunk in range(freq // 128):
                out_re[chunk, cut] = g_out[:, chunk * 128 : (chunk + 1) * 128]
                out_im[chunk, cut] = h_out[:, chunk * 128 : (chunk + 1) * 128]

        for k in range(GROUP):
            p = step * GROUP + k
            i = pairs[base + p, 0]
            j = pairs[base + p, 1]
            for chunk in range(freq // 128):
                cut = pl.ds(chunk * 128, 128)
                to_second = [None] * (4 * local)
                to_first = [None] * (4 * local)
                add = lambda total, term: term if total is None else total + term
                for c in range(part):
                    g = out_re[chunk, pl.ds(k * rows + c * part, part)]
                    h = out_im[chunk, pl.ds(k * rows + c * part, part)]
                    for w in range(2 * local):
                        a = first_row(k, i, w, 0, c, cut)
                        b = first_row(k, i, w, 1, c, cut)
                        to_second[2 * w] = add(to_second[2 * w], g * a - h * b)
                        to_second[2 * w + 1] = add(to_second[2 * w + 1], g * b + h * a)
                for w in range(2 * local):
                    for c in range(2):
                        add_to(j, w, c, second_part, cut, to_second[2 * w + c])
                for c in range(part):
                    g = out_re[chunk, pl.ds(k * rows + c, part, stride=part)]
                    h = out_im[chunk, pl.ds(k * rows + c, part, stride=part)]
                    for w in range(2 * local):
                        a = second_row(k, j, w, 0, c, cut)
                        b = second_row(k, j, w, 1, c, cut)
                        to_first[2 * w] = add(to_first[2 * w], g * a + h * b)
                        to_first[2 * w + 1] = add(to_first[2 * w + 1], g * b - h * a)
                for w in range(2 * local):
                    for c in range(2):
                        add_to(i, w, c, first_part, cut, to_first[2 * w + c])
        return carry

    lax.fori_loop(0, pair_count // GROUP, work, 0)

    if direct:
        count = len(HOPS[0])
        size = 2 * part
        for n in range(2 * count):
            index = meta[4 + n]
            target = own_grad if n < count else other_grad
            for w in range(2 * local):
                m = mask[w, index].astype(jnp.float32)
                for c in range(2):
                    to = pl.ds((((n % count) * 2 * local + w) * 2 + c) * size, size)
                    term = grad[index, w, c].reshape(size, freq) * m
                    target[to] = term.astype(target.dtype)
        other_grad[count * 4 * local * size :] = note_of(misfit[...], pair_count // 2)


def per_device(spectra, block_pairs, owners, window_mask):
    blk_count = lax.axis_size("blk")
    blk_index = lax.axis_index("blk")
    core = lax.axis_index("win")
    local = spectra.shape[0]
    channels = spectra.shape[3]
    freq = spectra.shape[4]
    part = channels // PARTS
    pair_total = block_pairs.shape[0]
    teams = blk_count // TEAM
    pair_count = pair_total // teams
    direct = teams == 1
    swap = [(0, 1), (1, 0)]
    smem = pl.BlockSpec(memory_space=pltpu.SMEM)
    vmem = pl.BlockSpec(memory_space=pltpu.VMEM)
    hbm = pl.BlockSpec(memory_space=pl.ANY)
    count = len(HOPS[0])
    hop_pairs = [
        [(2 * b + c, 2 * (b ^ HOPS[c][r]) + c) for b in range(TEAM) for c in range(2)]
        for r in range(count)
    ]
    meta = jnp.asarray(positions())[blk_index % TEAM, core]
    meta = meta.at[0].set(blk_index // TEAM * pair_count)

    owner_ids = owners[:, 0]
    order = jnp.arange(pair_total, dtype=jnp.int32)
    earlier = (owner_ids[:, None] == owner_ids[None, :]) & (order[None, :] < order[:, None])
    slot = owner_ids * CAP + jnp.sum(earlier.astype(jnp.int32), axis=1)
    mine_slots = blk_index * CAP + jnp.arange(CAP, dtype=jnp.int32)
    chosen = (slot[:, None] == mine_slots[None, :]).astype(jnp.float32)
    misfit_scale = 1.0 / (channels * channels * 2.0 * freq)

    if direct:
        other = lax.ppermute(spectra, "win", swap)
        parcel_type = jax.ShapeDtypeStruct((2 * local, 2, 2 * part, freq), jnp.bfloat16)
        parcels = pl.pallas_call(
            pack_kernel,
            out_shape=(parcel_type,) * count,
            in_specs=[smem, vmem, vmem],
            out_specs=(vmem,) * count,
            scratch_shapes=[pltpu.VMEM((PARTS, part, freq), jnp.float32)],
        )(meta, spectra, other)
        landed = [
            lax.ppermute(parcel, ("blk", "win"), pairs) for parcel, pairs in zip(parcels, hop_pairs)
        ]
        came = landed + [lax.ppermute(parcel, "win", swap) for parcel in landed]
    else:
        pieces = spectra[:, 0].reshape(local, 2, PARTS, part, freq)
        outgoing = jnp.stack(
            [jnp.stack([pieces[:, :, s] for s in SUBSETS[r]], axis=2) for r in range(TEAM)]
        ).reshape(TEAM, local, 2, 2 * part, freq)
        outgoing = jnp.tile(outgoing, (teams, 1, 1, 1, 1))
        own = lax.all_to_all(outgoing, "blk", split_axis=0, concat_axis=0, tiled=True)
        came = [own, lax.ppermute(own, "win", swap)]

    table_arrays = tables(freq)
    grad_shape = (blk_count, 2 * local, 2, 2 * part, freq)
    grad_bytes = math.prod(grad_shape) * 4
    rows = part * part * GROUP
    parcel_rows = 2 * local * 2 * 2 * part
    misfit_type = jax.ShapeDtypeStruct((pair_count, 128), jnp.float32)
    scratch = [
        pltpu.VMEM((GROUP * 4 * local, part, freq), jnp.float32),
        pltpu.VMEM((GROUP * 4 * local, part, freq), jnp.float32),
        pltpu.VMEM((rows, freq), jnp.bfloat16),
        pltpu.VMEM((rows, freq), jnp.bfloat16),
        pltpu.VMEM((rows, 2 * freq), jnp.bfloat16),
        pltpu.VMEM((freq // 128, rows, 128), jnp.float32),
        pltpu.VMEM((freq // 128, rows, 128), jnp.float32),
    ]
    scratch += [pltpu.VMEM(table.shape, jnp.bfloat16) for table in table_arrays[:4]]
    scratch += [pltpu.SemaphoreType.DMA((4,))]
    if direct:
        split_shape = (blk_count, 2 * local, 2, 2, part, freq)
        scratch += [pltpu.VMEM(split_shape, jnp.float32)] * 2
        out_types = (
            jax.ShapeDtypeStruct((count * parcel_rows, freq), jnp.float32),
            jax.ShapeDtypeStruct((count * parcel_rows + pair_count // 2, freq), jnp.bfloat16),
            misfit_type,
        )
    else:
        half = jax.ShapeDtypeStruct((blk_count, local, 2, 2 * part, freq), jnp.float32)
        out_types = (half, half, misfit_type)
    own_grad, other_grad, misfit = pl.pallas_call(
        functools.partial(pair_kernel, direct, pair_count),
        out_shape=out_types,
        in_specs=[smem] * 3 + [vmem] * len(came) + [hbm] * 4 + [vmem],
        out_specs=(vmem, vmem, vmem),
        scratch_shapes=scratch,
        compiler_params=pltpu.CompilerParams(
            vmem_limit_bytes=(16 << 20) + grad_bytes * 3 // (1 if direct else 2)
        ),
    )(meta, block_pairs, window_mask, *came, *table_arrays)

    if direct:
        swapped = lax.ppermute(other_grad, "win", swap)
        parcel_type = jax.ShapeDtypeStruct((parcel_rows + pair_count // 2, freq), jnp.bfloat16)
        parcels = pl.pallas_call(
            add_kernel,
            out_shape=(parcel_type,) * count,
            in_specs=[vmem] * 3,
            out_specs=(vmem,) * count,
        )(own_grad, swapped, misfit)
        landed = [
            lax.ppermute(parcel, ("blk", "win"), pairs) for parcel, pairs in zip(parcels, hop_pairs)
        ]
        half_type = jax.ShapeDtypeStruct((local * 2 * channels + pair_count, freq), jnp.float32)
        mine, give = pl.pallas_call(
            merge_kernel,
            out_shape=(half_type, half_type),
            in_specs=[smem] + [vmem] * count,
            out_specs=(vmem, vmem),
            scratch_shapes=[pltpu.VMEM((2 * local, 2, PARTS, part, freq), jnp.float32)],
        )(meta, *landed)
        swapped = lax.ppermute(give, "win", swap)
        gradient, totals = pl.pallas_call(
            functools.partial(finish_kernel, scale=misfit_scale),
            out_shape=(
                jax.ShapeDtypeStruct(spectra.shape, jnp.bfloat16),
                jax.ShapeDtypeStruct((1, CAP), jnp.float32),
            ),
            in_specs=[vmem] * 3,
            out_specs=(vmem, vmem),
        )(mine, swapped, chosen)
        return (gradient, totals.reshape(CAP))

    swapped = lax.ppermute(other_grad.astype(jnp.bfloat16), "win", swap)
    terms = jnp.sum(misfit, axis=1)
    terms = terms + lax.ppermute(terms, "win", swap)
    chip_grad = (own_grad + swapped.astype(jnp.float32)).astype(jnp.bfloat16)
    high = terms.astype(jnp.bfloat16)
    low = (terms - high.astype(jnp.float32)).astype(jnp.bfloat16)
    note = jnp.zeros((8, freq), jnp.bfloat16).at[0, :pair_count].set(high).at[1, :pair_count].set(low)
    grad_rows = local * 2 * 2 * part
    payload = jnp.concatenate(
        [
            chip_grad.reshape(blk_count, grad_rows, freq),
            jnp.broadcast_to(note[None], (blk_count, 8, freq)),
        ],
        axis=1,
    )
    arrived = lax.all_to_all(payload, "blk", split_axis=0, concat_axis=0, tiled=True)
    wide = arrived[:, :grad_rows].reshape(teams, TEAM, local, 2, 2, part, freq).astype(jnp.float32)
    wide = jnp.sum(wide, axis=0)
    gradient = jnp.stack(
        [
            sum(wide[r, :, :, SUBSETS[r].index(s)] for r in range(TEAM) if s in SUBSETS[r])
            for s in range(PARTS)
        ],
        axis=2,
    )
    gradient = gradient.reshape(local, 1, 2, channels, freq).astype(jnp.bfloat16)
    notes = arrived[:, grad_rows:, :pair_count].astype(jnp.float32)
    notes = jnp.sum((notes[:, 0] + notes[:, 1]).reshape(teams, TEAM, pair_count), axis=1)
    pair_misfit = notes.reshape(pair_total) * misfit_scale
    totals = jnp.sum(pair_misfit[:, None] * chosen, axis=0)
    return (gradient, totals)


def solution(mesh):
    return jax.shard_map(
        per_device,
        mesh=mesh,
        in_specs=(
            P("win", ("groups", "blk"), None, None, None),
            P("groups", None),
            P("groups", None),
            P(None, "groups"),
        ),
        out_specs=(P("win", ("groups", "blk"), None, None, None), P(("groups", "blk"))),
        check_vma=False,
    )
```

```python
import functools
import math

import jax
import jax.numpy as jnp
import ml_dtypes
import numpy as np
from jax import lax
from jax.experimental import pallas as pl
from jax.experimental.pallas import tpu as pltpu
from jax.sharding import PartitionSpec as P

CAP = 3
PARTS = 4
TEAM = 8
SUBSETS = ((0, 1), (0, 1), (0, 2), (0, 3), (1, 2), (1, 3), (2, 3), (2, 3))
GROUP = 4
SMALL_VMEM = 6 << 20
HOPS = ((6, 4, 2, 0), (7, 5, 3, 1))


@functools.lru_cache(maxsize=None)
def tables(freq_count):
    lag_count = 2 * freq_count
    f = np.arange(freq_count)[:, None]
    t = np.arange(freq_count)[None, :]
    phase = (f * t % lag_count) * (2.0 * np.pi / lag_count)
    cos = np.cos(phase)
    sin = -np.sin(phase)
    alternate = np.where(np.arange(freq_count) % 2 == 0, 1.0, -1.0)
    extra = np.zeros((freq_count, 128))
    extra[:, 0] = alternate
    forward_re = np.concatenate([cos, extra], axis=1)
    cos_back = cos.T
    cos_mirror = cos_back.copy()
    cos_mirror[0] = alternate
    back_re = np.concatenate([cos_back, cos_mirror], axis=0)
    back_im = np.concatenate([sin.T, -sin.T], axis=0)
    taper = 1.0 + np.cos(np.pi * np.arange(lag_count) / lag_count)
    mirror = np.concatenate([[freq_count], lag_count - np.arange(1, freq_count)])
    weight = np.stack([taper[:freq_count], taper[mirror]]) / 8.0
    as_bf16 = lambda x: x.astype(np.float32).astype(ml_dtypes.bfloat16)
    return (
        as_bf16(forward_re),
        as_bf16(sin),
        as_bf16(back_re),
        as_bf16(back_im),
        weight.astype(np.float32),
    )


@functools.lru_cache(maxsize=None)
def positions():
    out = np.zeros((TEAM, 2, 20), np.int32)
    for rank in range(TEAM):
        for core in range(2):
            same = rank in (0, TEAM - 1)
            row = [0, core, core if same else 1 - core, core]
            row += [rank ^ hop for hop in HOPS[core]]
            row += [rank ^ hop for hop in HOPS[1 - core]]
            for hop in HOPS[core]:
                row += SUBSETS[rank ^ hop]
            out[rank, core] = row
    return out.reshape(TEAM * 2, -1)


def pack_kernel(meta, own, other, *refs):
    parcels, wide = refs[:-1], refs[-1]
    local = own.shape[0]
    core = meta[3]
    for source, side in ((own, core), (other, 1 - core)):
        for w in range(local):
            for c in range(2):
                wide[...] = source[w, 0, c].astype(jnp.float32).reshape(wide.shape)
                for r, parcel in enumerate(parcels):
                    both = [wide[meta[12 + 2 * r + n]] for n in range(2)]
                    parcel[side * local + w, c] = jnp.concatenate(both, axis=0).astype(jnp.bfloat16)


def add_kernel(keep, came, terms, *parcels):
    count = len(parcels)
    rows = keep.shape[0] // count
    pair_count = terms.shape[0]
    half = pair_count // 2
    arrived = came[count * rows :].astype(jnp.float32)
    total = terms[...] + jnp.concatenate(
        [arrived[:, :128] + arrived[:, 256:384], arrived[:, 128:256] + arrived[:, 384:512]], axis=0
    )
    note = note_of(total, half)
    for r, parcel in enumerate(parcels):
        cut = slice(r * rows, (r + 1) * rows)
        parcel[:rows] = (keep[cut] + came[cut].astype(jnp.float32)).astype(jnp.bfloat16)
        parcel[rows:] = note


def note_of(total, half):
    high = total.astype(jnp.bfloat16).astype(jnp.float32)
    low = total - high
    return jnp.concatenate([high[:half], high[half:], low[:half], low[half:]], axis=1).astype(
        jnp.bfloat16
    )


def merge_kernel(meta, *refs):
    parcels, (mine, give, total) = refs[: len(HOPS[0])], refs[len(HOPS[0]) :]
    windows, _, _, part, freq = total.shape
    channels = PARTS * part
    local = windows // 2
    core = meta[3]
    rows = windows * 2 * 2 * part
    note = None
    total[...] = jnp.zeros_like(total)
    for r, parcel in enumerate(parcels):
        for w in range(windows):
            for c in range(2):
                for n in range(2):
                    start = ((w * 2 + c) * 2 + n) * part
                    term = parcel[start : start + part].astype(jnp.float32)
                    total[w, c, meta[12 + 2 * r + n]] += term
        tail = parcel[rows:].astype(jnp.float32)
        tail = jnp.concatenate(
            [tail[:, :128] + tail[:, 256:384], tail[:, 128:256] + tail[:, 384:512]], axis=0
        )
        note = tail if note is None else note + tail
    for w in range(local):
        for c in range(2):
            to = slice((w * 2 + c) * channels, (w * 2 + c + 1) * channels)
            mine[to] = total[core * local + w, c].reshape(channels, freq)
            give[to] = total[(1 - core) * local + w, c].reshape(channels, freq)
    body = local * 2 * channels
    pad = jnp.zeros((note.shape[0], freq - 128), jnp.float32)
    mine[body:] = jnp.concatenate([note, pad], axis=1)
    give[body:] = jnp.concatenate([note, pad], axis=1)


def finish_kernel(mine, came, chosen, gradient, totals, scale):
    local, _, _, channels, _ = gradient.shape
    for w in range(local):
        for c in range(2):
            cut = slice((w * 2 + c) * channels, (w * 2 + c + 1) * channels)
            gradient[w, 0, c] = (mine[cut] + came[cut]).astype(jnp.bfloat16)
    body = local * 2 * channels
    note = mine[body:, :128] + came[body:, :128]
    pair = jnp.sum(note, axis=1, keepdims=True) * scale
    totals[...] = jnp.sum(pair * chosen[...], axis=0, keepdims=True)


def pair_kernel(
    direct,
    pair_count,
    meta,
    pairs,
    mask,
    *refs,
):
    sources = 2 * len(HOPS[0]) if direct else 2
    came, refs = refs[:sources], refs[sources:]
    (
        forward_re_hbm,
        forward_im_hbm,
        back_re_hbm,
        back_im_hbm,
        weight,
        own_grad,
        other_grad,
        misfit,
        first,
        second,
        cross_re,
        cross_im,
        adj,
        out_re,
        out_im,
        forward_re,
        forward_im,
        back_re,
        back_im,
        sems,
    ) = refs[:20]
    copies = [
        pltpu.make_async_copy(source, target, sems.at[n])
        for n, (source, target) in enumerate(
            (
                (forward_re_hbm, forward_re),
                (forward_im_hbm, forward_im),
                (back_re_hbm, back_re),
                (back_im_hbm, back_im),
            )
        )
    ]
    for copy in copies:
        copy.start()
    freq = came[0].shape[-1]
    part = came[0].shape[-2] // 2
    local = mask.shape[0] // 2
    base = meta[0]
    first_part = meta[1]
    second_part = meta[2]
    core = meta[3]
    rows = part * part
    lanes = 256

    if direct:
        field, grad = refs[20:]
        for n, parcel in enumerate(came):
            index = meta[4 + n]
            for w in range(2 * local):
                m = mask[w, index].astype(jnp.float32)
                for c in range(2):
                    field[index, w, c] = (parcel[w, c].astype(jnp.float32) * m).reshape(2, part, freq)
        grad[...] = jnp.zeros_like(grad)
    else:
        own_grad[...] = jnp.zeros_like(own_grad)
        other_grad[...] = jnp.zeros_like(other_grad)

    def block(index, w, c, which):
        both = came[w // local][index, w % local, c].astype(jnp.float32)
        return jnp.where(which == 0, both[:part], both[part:])

    def first_row(k, i, w, c, row, cut):
        if direct:
            return field[i, w, c, first_part, pl.ds(row, 1), cut]
        return first[(k * 2 * local + w) * 2 + c, pl.ds(row, 1), cut]

    def second_row(k, j, w, c, row, cut):
        if direct:
            return field[j, w, c, second_part, pl.ds(row, 1), cut]
        return second[(k * 2 * local + w) * 2 + c, pl.ds(row, 1), cut]

    def add_to(index, w, c, which, cut, term):
        if direct:
            grad[index, w, c, which, :, cut] += term
        else:
            target = own_grad if w < local else other_grad
            target[index, w % local, c, pl.ds(which * part, part), cut] += term

    def work(step, carry):
        counts = []
        for k in range(GROUP):
            p = step * GROUP + k
            i = pairs[base + p, 0]
            j = pairs[base + p, 1]
            shared = jnp.int32(0)
            for w in range(2 * local):
                side = core if w < local else 1 - core
                where = w if direct else side * local + w % local
                m = mask[where, i] * mask[where, j]
                shared = shared + m
                if direct:
                    continue
                m = m.astype(jnp.float32)
                for c in range(2):
                    at = k * 4 * local + w * 2 + c
                    first[at] = block(i, w, c, first_part) * m
                    second[at] = block(j, w, c, second_part) * m
            counts.append(jnp.maximum(shared, 1).astype(jnp.float32) * (2.0 * freq))
            for chunk in range(freq // lanes):
                cut = pl.ds(chunk * lanes, lanes)
                if direct:
                    right = [field[j, n // 2, n % 2, second_part, :, cut] for n in range(4 * local)]
                else:
                    right = [second[k * 4 * local + n, :, cut] for n in range(4 * local)]
                for c1 in range(part):
                    re = None
                    for w in range(2 * local):
                        a = first_row(k, i, w, 0, c1, cut)
                        b = first_row(k, i, w, 1, c1, cut)
                        aa = a * right[2 * w] + b * right[2 * w + 1]
                        ab = a * right[2 * w + 1] - b * right[2 * w]
                        re = aa if re is None else re + aa
                        im = ab if w == 0 else im + ab
                    cross_re[pl.ds(k * rows + c1 * part, part), cut] = re.astype(jnp.bfloat16)
                    cross_im[pl.ds(k * rows + c1 * part, part), cut] = im.astype(jnp.bfloat16)

        @pl.when(step == 0)
        def _():
            for copy in copies:
                copy.wait()

        cos_sum = jnp.dot(cross_re[...], forward_re[...], preferred_element_type=jnp.float32)
        sin_sum = jnp.dot(cross_im[...], forward_im[...], preferred_element_type=jnp.float32)
        lane = lax.broadcasted_iota(jnp.int32, (rows, freq), 1)
        for k in range(GROUP):
            cut = slice(k * rows, (k + 1) * rows)
            scale = 0.5 * lax.rsqrt(jnp.full((1, freq), counts[k], jnp.float32))
            even = cos_sum[cut, :freq] * scale
            odd = sin_sum[cut] * (3.0 * scale)
            middle = cos_sum[cut, freq : freq + 1] * scale
            plus = even + odd
            minus = jnp.where(lane == 0, middle, even - odd)
            plus_adj = plus * plus * plus * weight[0:1, :]
            minus_adj = minus * minus * minus * weight[1:2, :]
            adj[cut, :freq] = plus_adj.astype(jnp.bfloat16)
            adj[cut, freq:] = minus_adj.astype(jnp.bfloat16)
            total = plus_adj * plus + minus_adj * minus
            total = jnp.sum(total, axis=0, keepdims=True)
            total = sum(total[:, n : n + 128] for n in range(0, freq, 128))
            misfit[pl.ds(step * GROUP + k, 1), :] = total
        g_sum = jnp.dot(adj[...], back_re[...], preferred_element_type=jnp.float32)
        h_sum = jnp.dot(adj[...], back_im[...], preferred_element_type=jnp.float32)
        for k in range(GROUP):
            cut = slice(k * rows, (k + 1) * rows)
            scale = lax.rsqrt(jnp.full((1, freq), counts[k] * (4.0 * part), jnp.float32))
            g_out = (g_sum[cut] * scale).astype(jnp.bfloat16).astype(jnp.float32)
            h_out = (h_sum[cut] * scale).astype(jnp.bfloat16).astype(jnp.float32)
            for chunk in range(freq // 128):
                out_re[chunk, cut] = g_out[:, chunk * 128 : (chunk + 1) * 128]
                out_im[chunk, cut] = h_out[:, chunk * 128 : (chunk + 1) * 128]

        for k in range(GROUP):
            p = step * GROUP + k
            i = pairs[base + p, 0]
            j = pairs[base + p, 1]
            for chunk in range(freq // 128):
                cut = pl.ds(chunk * 128, 128)
                to_second = [None] * (4 * local)
                to_first = [None] * (4 * local)
                add = lambda total, term: term if total is None else total + term
                for c in range(part):
                    g = out_re[chunk, pl.ds(k * rows + c * part, part)]
                    h = out_im[chunk, pl.ds(k * rows + c * part, part)]
                    for w in range(2 * local):
                        a = first_row(k, i, w, 0, c, cut)
                        b = first_row(k, i, w, 1, c, cut)
                        to_second[2 * w] = add(to_second[2 * w], g * a - h * b)
                        to_second[2 * w + 1] = add(to_second[2 * w + 1], g * b + h * a)
                for w in range(2 * local):
                    for c in range(2):
                        add_to(j, w, c, second_part, cut, to_second[2 * w + c])
                for c in range(part):
                    g = out_re[chunk, pl.ds(k * rows + c, part, stride=part)]
                    h = out_im[chunk, pl.ds(k * rows + c, part, stride=part)]
                    for w in range(2 * local):
                        a = second_row(k, j, w, 0, c, cut)
                        b = second_row(k, j, w, 1, c, cut)
                        to_first[2 * w] = add(to_first[2 * w], g * a + h * b)
                        to_first[2 * w + 1] = add(to_first[2 * w + 1], g * b - h * a)
                for w in range(2 * local):
                    for c in range(2):
                        add_to(i, w, c, first_part, cut, to_first[2 * w + c])
        return carry

    lax.fori_loop(0, pair_count // GROUP, work, 0)

    if direct:
        count = len(HOPS[0])
        size = 2 * part
        for n in range(2 * count):
            index = meta[4 + n]
            target = own_grad if n < count else other_grad
            for w in range(2 * local):
                m = mask[w, index].astype(jnp.float32)
                for c in range(2):
                    to = pl.ds((((n % count) * 2 * local + w) * 2 + c) * size, size)
                    term = grad[index, w, c].reshape(size, freq) * m
                    target[to] = term.astype(target.dtype)
        other_grad[count * 4 * local * size :] = note_of(misfit[...], pair_count // 2)


def per_device(spectra, block_pairs, owners, window_mask):
    blk_count = lax.axis_size("blk")
    blk_index = lax.axis_index("blk")
    core = lax.axis_index("win")
    local = spectra.shape[0]
    channels = spectra.shape[3]
    freq = spectra.shape[4]
    part = channels // PARTS
    pair_total = block_pairs.shape[0]
    teams = blk_count // TEAM
    pair_count = pair_total // teams
    direct = teams == 1
    swap = [(0, 1), (1, 0)]
    smem = pl.BlockSpec(memory_space=pltpu.SMEM)
    vmem = pl.BlockSpec(memory_space=pltpu.VMEM)
    hbm = pl.BlockSpec(memory_space=pltpu.HBM)
    small = pltpu.CompilerParams(vmem_limit_bytes=SMALL_VMEM)
    count = len(HOPS[0])
    hop_pairs = [
        [(2 * b + c, 2 * (b ^ HOPS[c][r]) + c) for b in range(TEAM) for c in range(2)]
        for r in range(count)
    ]
    rank = blk_index if direct else lax.rem(blk_index, TEAM)
    meta = lax.dynamic_slice_in_dim(jnp.asarray(positions()), rank * 2 + core, 1)[0]
    if not direct:
        meta = meta.at[0].set(lax.div(blk_index, TEAM) * pair_count)

    owner_ids = owners[:, 0]
    order = jnp.arange(pair_total, dtype=jnp.int32)
    earlier = (owner_ids[:, None] == owner_ids[None, :]) & (order[None, :] < order[:, None])
    slot = owner_ids * CAP + jnp.sum(earlier.astype(jnp.int32), axis=1)
    mine_slots = blk_index * CAP + jnp.arange(CAP, dtype=jnp.int32)
    chosen = (slot[:, None] == mine_slots[None, :]).astype(jnp.float32)
    misfit_scale = 1.0 / (channels * channels * 2.0 * freq)

    table_arrays = [jnp.asarray(table) for table in tables(freq)]
    table_arrays[:4] = [
        pltpu.with_memory_space_constraint(table, pltpu.HBM) for table in table_arrays[:4]
    ]
    if direct:
        other = lax.ppermute(spectra, "win", swap)
        parcel_type = jax.ShapeDtypeStruct((2 * local, 2, 2 * part, freq), jnp.bfloat16)
        parcels = pl.pallas_call(
            pack_kernel,
            out_shape=(parcel_type,) * count,
            in_specs=[smem, vmem, vmem],
            out_specs=(vmem,) * count,
            scratch_shapes=[pltpu.VMEM((PARTS, part, freq), jnp.float32)],
            compiler_params=small,
        )(meta, spectra, other)
        landed = [
            lax.ppermute(parcel, ("blk", "win"), pairs) for parcel, pairs in zip(parcels, hop_pairs)
        ]
        came = landed + [lax.ppermute(parcel, "win", swap) for parcel in landed]
    else:
        pieces = spectra[:, 0].reshape(local, 2, PARTS, part, freq)
        outgoing = jnp.stack(
            [jnp.stack([pieces[:, :, s] for s in SUBSETS[r]], axis=2) for r in range(TEAM)]
        ).reshape(TEAM, local, 2, 2 * part, freq)
        outgoing = jnp.tile(outgoing, (teams, 1, 1, 1, 1))
        own = lax.all_to_all(outgoing, "blk", split_axis=0, concat_axis=0, tiled=True)
        came = [own, lax.ppermute(own, "win", swap)]

    grad_shape = (blk_count, 2 * local, 2, 2 * part, freq)
    grad_bytes = math.prod(grad_shape) * 4
    rows = part * part * GROUP
    parcel_rows = 2 * local * 2 * 2 * part
    misfit_type = jax.ShapeDtypeStruct((pair_count, 128), jnp.float32)
    scratch = [
        pltpu.VMEM((GROUP * 4 * local, part, freq), jnp.float32),
        pltpu.VMEM((GROUP * 4 * local, part, freq), jnp.float32),
        pltpu.VMEM((rows, freq), jnp.bfloat16),
        pltpu.VMEM((rows, freq), jnp.bfloat16),
        pltpu.VMEM((rows, 2 * freq), jnp.bfloat16),
        pltpu.VMEM((freq // 128, rows, 128), jnp.float32),
        pltpu.VMEM((freq // 128, rows, 128), jnp.float32),
    ]
    scratch += [pltpu.VMEM(table.shape, jnp.bfloat16) for table in table_arrays[:4]]
    scratch += [pltpu.SemaphoreType.DMA((4,))]
    if direct:
        split_shape = (blk_count, 2 * local, 2, 2, part, freq)
        scratch += [pltpu.VMEM(split_shape, jnp.float32)] * 2
        out_types = (
            jax.ShapeDtypeStruct((count * parcel_rows, freq), jnp.float32),
            jax.ShapeDtypeStruct((count * parcel_rows + pair_count // 2, freq), jnp.bfloat16),
            misfit_type,
        )
    else:
        half = jax.ShapeDtypeStruct((blk_count, local, 2, 2 * part, freq), jnp.float32)
        out_types = (half, half, misfit_type)
    own_grad, other_grad, misfit = pl.pallas_call(
        functools.partial(pair_kernel, direct, pair_count),
        out_shape=out_types,
        in_specs=[smem] * 3 + [vmem] * len(came) + [hbm] * 4 + [vmem],
        out_specs=(vmem, vmem, vmem),
        scratch_shapes=scratch,
        compiler_params=pltpu.CompilerParams(
            vmem_limit_bytes=(16 << 20) + grad_bytes * 3 // (1 if direct else 2)
        ),
    )(meta, block_pairs, window_mask, *came, *table_arrays)

    if direct:
        swapped = lax.ppermute(other_grad, "win", swap)
        parcel_type = jax.ShapeDtypeStruct((parcel_rows + pair_count // 2, freq), jnp.bfloat16)
        parcels = pl.pallas_call(
            add_kernel,
            out_shape=(parcel_type,) * count,
            in_specs=[vmem] * 3,
            out_specs=(vmem,) * count,
            compiler_params=small,
        )(own_grad, swapped, misfit)
        landed = [
            lax.ppermute(parcel, ("blk", "win"), pairs) for parcel, pairs in zip(parcels, hop_pairs)
        ]
        half_type = jax.ShapeDtypeStruct((local * 2 * channels + pair_count, freq), jnp.float32)
        mine, give = pl.pallas_call(
            merge_kernel,
            out_shape=(half_type, half_type),
            in_specs=[smem] + [vmem] * count,
            out_specs=(vmem, vmem),
            scratch_shapes=[pltpu.VMEM((2 * local, 2, PARTS, part, freq), jnp.float32)],
            compiler_params=small,
        )(meta, *landed)
        swapped = lax.ppermute(give, "win", swap)
        gradient, totals = pl.pallas_call(
            functools.partial(finish_kernel, scale=misfit_scale),
            out_shape=(
                jax.ShapeDtypeStruct(spectra.shape, jnp.bfloat16),
                jax.ShapeDtypeStruct((1, CAP), jnp.float32),
            ),
            in_specs=[vmem] * 3,
            out_specs=(vmem, vmem),
            compiler_params=small,
        )(mine, swapped, chosen)
        return (gradient, totals.reshape(CAP))

    swapped = lax.ppermute(other_grad.astype(jnp.bfloat16), "win", swap)
    terms = jnp.sum(misfit, axis=1)
    terms = terms + lax.ppermute(terms, "win", swap)
    chip_grad = (own_grad + swapped.astype(jnp.float32)).astype(jnp.bfloat16)
    high = terms.astype(jnp.bfloat16)
    low = (terms - high.astype(jnp.float32)).astype(jnp.bfloat16)
    note = jnp.zeros((8, freq), jnp.bfloat16).at[0, :pair_count].set(high).at[1, :pair_count].set(low)
    grad_rows = local * 2 * 2 * part
    payload = jnp.concatenate(
        [
            chip_grad.reshape(blk_count, grad_rows, freq),
            jnp.broadcast_to(note[None], (blk_count, 8, freq)),
        ],
        axis=1,
    )
    arrived = lax.all_to_all(payload, "blk", split_axis=0, concat_axis=0, tiled=True)
    wide = arrived[:, :grad_rows].reshape(teams, TEAM, local, 2, 2, part, freq).astype(jnp.float32)
    wide = jnp.sum(wide, axis=0)
    gradient = jnp.stack(
        [
            sum(wide[r, :, :, SUBSETS[r].index(s)] for r in range(TEAM) if s in SUBSETS[r])
            for s in range(PARTS)
        ],
        axis=2,
    )
    gradient = gradient.reshape(local, 1, 2, channels, freq).astype(jnp.bfloat16)
    notes = arrived[:, grad_rows:, :pair_count].astype(jnp.float32)
    notes = jnp.sum((notes[:, 0] + notes[:, 1]).reshape(teams, TEAM, pair_count), axis=1)
    pair_misfit = notes.reshape(pair_total) * misfit_scale
    totals = jnp.sum(pair_misfit[:, None] * chosen, axis=0)
    return (gradient, totals)


def solution(mesh):
    return jax.shard_map(
        per_device,
        mesh=mesh,
        in_specs=(
            P("win", ("groups", "blk"), None, None, None),
            P("groups", None),
            P("groups", None),
            P(None, "groups"),
        ),
        out_specs=(P("win", ("groups", "blk"), None, None, None), P(("groups", "blk"))),
        check_vma=False,
    )
```

```python
import functools
import math

import jax
import jax.numpy as jnp
import ml_dtypes
import numpy as np
from jax import lax
from jax.experimental import pallas as pl
from jax.experimental.pallas import tpu as pltpu
from jax.sharding import PartitionSpec as P

CAP = 3
PARTS = 4
TEAM = 8
SUBSETS = ((0, 1), (0, 1), (0, 2), (0, 3), (1, 2), (1, 3), (2, 3), (2, 3))
GROUP = 4
SMALL_VMEM = 6 << 20
HOPS = ((6, 4, 2, 0), (7, 5, 3, 1))


@functools.lru_cache(maxsize=None)
def tables(freq_count):
    lag_count = 2 * freq_count
    f = np.arange(freq_count)[:, None]
    t = np.arange(freq_count)[None, :]
    phase = (f * t % lag_count) * (2.0 * np.pi / lag_count)
    cos = np.cos(phase)
    sin = -np.sin(phase)
    alternate = np.where(np.arange(freq_count) % 2 == 0, 1.0, -1.0)
    extra = np.zeros((freq_count, 128))
    extra[:, 0] = alternate
    forward_re = np.concatenate([cos, extra], axis=1)
    cos_back = cos.T
    cos_mirror = cos_back.copy()
    cos_mirror[0] = alternate
    back_re = np.concatenate([cos_back, cos_mirror], axis=0)
    back_im = np.concatenate([sin.T, -sin.T], axis=0)
    taper = 1.0 + np.cos(np.pi * np.arange(lag_count) / lag_count)
    mirror = np.concatenate([[freq_count], lag_count - np.arange(1, freq_count)])
    weight = np.stack([taper[:freq_count], taper[mirror]]) / 8.0
    as_bf16 = lambda x: x.astype(np.float32).astype(ml_dtypes.bfloat16)
    return (
        as_bf16(forward_re),
        as_bf16(sin),
        as_bf16(back_re),
        as_bf16(back_im),
        weight.astype(np.float32),
    )


@functools.lru_cache(maxsize=None)
def positions():
    out = np.zeros((TEAM, 2, 20), np.int32)
    for rank in range(TEAM):
        for core in range(2):
            same = rank in (0, TEAM - 1)
            row = [0, core, core if same else 1 - core, core]
            row += [rank ^ hop for hop in HOPS[core]]
            row += [rank ^ hop for hop in HOPS[1 - core]]
            for hop in HOPS[core]:
                row += SUBSETS[rank ^ hop]
            out[rank, core] = row
    return out.reshape(TEAM * 2, -1)


def team_tables(freq_count):
    forward_re, forward_im, _, _, weight = tables(freq_count)
    turn = np.broadcast_to(forward_re[:, freq_count : freq_count + 1], (freq_count, 128))
    in_hbm = [
        pltpu.with_memory_space_constraint(jnp.asarray(table), pltpu.HBM)
        for table in (forward_re[:, :freq_count], forward_im)
    ]
    return (*in_hbm, jnp.asarray(turn), jnp.asarray(weight))


def pack_kernel(meta, own, other, *refs):
    parcels, wide = refs[:-1], refs[-1]
    local = own.shape[0]
    core = meta[3]
    for source, side in ((own, core), (other, 1 - core)):
        for w in range(local):
            for c in range(2):
                wide[...] = source[w, 0, c].astype(jnp.float32).reshape(wide.shape)
                for r, parcel in enumerate(parcels):
                    both = [wide[meta[12 + 2 * r + n]] for n in range(2)]
                    parcel[side * local + w, c] = jnp.concatenate(both, axis=0).astype(jnp.bfloat16)


def add_kernel(keep, came, terms, *parcels):
    count = len(parcels)
    rows = keep.shape[0] // count
    pair_count = terms.shape[0]
    half = pair_count // 2
    arrived = came[count * rows :].astype(jnp.float32)
    total = terms[...] + jnp.concatenate(
        [arrived[:, :128] + arrived[:, 256:384], arrived[:, 128:256] + arrived[:, 384:512]], axis=0
    )
    note = note_of(total, half)
    for r, parcel in enumerate(parcels):
        cut = slice(r * rows, (r + 1) * rows)
        parcel[:rows] = (keep[cut] + came[cut].astype(jnp.float32)).astype(jnp.bfloat16)
        parcel[rows:] = note


def note_of(total, half):
    high = total.astype(jnp.bfloat16).astype(jnp.float32)
    low = total - high
    return jnp.concatenate([high[:half], high[half:], low[:half], low[half:]], axis=1).astype(
        jnp.bfloat16
    )


def merge_kernel(meta, *refs):
    parcels, (mine, give, total) = refs[: len(HOPS[0])], refs[len(HOPS[0]) :]
    windows, _, _, part, freq = total.shape
    channels = PARTS * part
    local = windows // 2
    core = meta[3]
    rows = windows * 2 * 2 * part
    note = None
    total[...] = jnp.zeros_like(total)
    for r, parcel in enumerate(parcels):
        for w in range(windows):
            for c in range(2):
                for n in range(2):
                    start = ((w * 2 + c) * 2 + n) * part
                    term = parcel[start : start + part].astype(jnp.float32)
                    total[w, c, meta[12 + 2 * r + n]] += term
        tail = parcel[rows:].astype(jnp.float32)
        tail = jnp.concatenate(
            [tail[:, :128] + tail[:, 256:384], tail[:, 128:256] + tail[:, 384:512]], axis=0
        )
        note = tail if note is None else note + tail
    for w in range(local):
        for c in range(2):
            to = slice((w * 2 + c) * channels, (w * 2 + c + 1) * channels)
            mine[to] = total[core * local + w, c].reshape(channels, freq)
            give[to] = total[(1 - core) * local + w, c].reshape(channels, freq)
    body = local * 2 * channels
    pad = jnp.zeros((note.shape[0], freq - 128), jnp.float32)
    mine[body:] = jnp.concatenate([note, pad], axis=1)
    give[body:] = jnp.concatenate([note, pad], axis=1)


def finish_kernel(mine, came, chosen, gradient, totals, scale):
    local, _, _, channels, _ = gradient.shape
    for w in range(local):
        for c in range(2):
            cut = slice((w * 2 + c) * channels, (w * 2 + c + 1) * channels)
            gradient[w, 0, c] = (mine[cut] + came[cut]).astype(jnp.bfloat16)
    body = local * 2 * channels
    note = mine[body:, :128] + came[body:, :128]
    pair = jnp.sum(note, axis=1, keepdims=True) * scale
    totals[...] = jnp.sum(pair * chosen[...], axis=0, keepdims=True)


def pair_kernel(
    meta,
    pairs,
    mask,
    own,
    other,
    forward_re,
    forward_im,
    back_re,
    back_im,
    weight,
    own_grad,
    other_grad,
    misfit,
    first,
    second,
    cross_re,
    cross_im,
    adj,
    out_re,
    out_im,
):
    pair_count = misfit.shape[0]
    freq = own.shape[-1]
    part = own.shape[3] // 2
    local = own.shape[1]
    base = meta[0]
    first_part = meta[1]
    second_part = meta[2]
    core = meta[3]
    rows = part * part
    lanes = 256

    own_grad[...] = jnp.zeros_like(own_grad)
    other_grad[...] = jnp.zeros_like(other_grad)

    def block(source, index, w, c, which):
        both = source[index, w, c].astype(jnp.float32)
        return jnp.where(which == 0, both[:part], both[part:])

    def work(step, carry):
        counts = []
        for k in range(GROUP):
            p = step * GROUP + k
            i = pairs[base + p, 0]
            j = pairs[base + p, 1]
            shared = jnp.int32(0)
            for w in range(2 * local):
                is_own = w < local
                source = own if is_own else other
                side = core if is_own else 1 - core
                where = side * local + w % local
                m = mask[where, i] * mask[where, j]
                shared = shared + m
                m = m.astype(jnp.float32)
                for c in range(2):
                    at = k * 4 * local + w * 2 + c
                    first[at] = block(source, i, w % local, c, first_part) * m
                    second[at] = block(source, j, w % local, c, second_part) * m
            counts.append(jnp.maximum(shared, 1).astype(jnp.float32) * (2.0 * freq))
            for chunk in range(freq // lanes):
                cut = pl.ds(chunk * lanes, lanes)
                right = [second[k * 4 * local + n, :, cut] for n in range(4 * local)]
                for c1 in range(part):
                    re = None
                    for w in range(2 * local):
                        a = first[k * 4 * local + 2 * w, pl.ds(c1, 1), cut]
                        b = first[k * 4 * local + 2 * w + 1, pl.ds(c1, 1), cut]
                        aa = a * right[2 * w] + b * right[2 * w + 1]
                        ab = a * right[2 * w + 1] - b * right[2 * w]
                        re = aa if re is None else re + aa
                        im = ab if w == 0 else im + ab
                    cross_re[pl.ds(k * rows + c1 * part, part), cut] = re.astype(jnp.bfloat16)
                    cross_im[pl.ds(k * rows + c1 * part, part), cut] = im.astype(jnp.bfloat16)

        cos_sum = jnp.dot(cross_re[...], forward_re[...], preferred_element_type=jnp.float32)
        sin_sum = jnp.dot(cross_im[...], forward_im[...], preferred_element_type=jnp.float32)
        lane = lax.broadcasted_iota(jnp.int32, (rows, freq), 1)
        for k in range(GROUP):
            cut = slice(k * rows, (k + 1) * rows)
            scale = 0.5 * lax.rsqrt(jnp.full((1, freq), counts[k], jnp.float32))
            even = cos_sum[cut, :freq] * scale
            odd = sin_sum[cut] * (3.0 * scale)
            middle = cos_sum[cut, freq : freq + 1] * scale
            plus = even + odd
            minus = jnp.where(lane == 0, middle, even - odd)
            plus_adj = plus * plus * plus * weight[0:1, :]
            minus_adj = minus * minus * minus * weight[1:2, :]
            adj[cut, :freq] = plus_adj.astype(jnp.bfloat16)
            adj[cut, freq:] = minus_adj.astype(jnp.bfloat16)
            total = plus_adj * plus + minus_adj * minus
            misfit[pl.ds(step * GROUP + k, 1), :] = jnp.sum(total, axis=0, keepdims=True)
        g_sum = jnp.dot(adj[...], back_re[...], preferred_element_type=jnp.float32)
        h_sum = jnp.dot(adj[...], back_im[...], preferred_element_type=jnp.float32)
        for k in range(GROUP):
            cut = slice(k * rows, (k + 1) * rows)
            scale = lax.rsqrt(jnp.full((1, freq), counts[k] * (4.0 * part), jnp.float32))
            g_out = (g_sum[cut] * scale).astype(jnp.bfloat16).astype(jnp.float32)
            h_out = (h_sum[cut] * scale).astype(jnp.bfloat16).astype(jnp.float32)
            for chunk in range(freq // 128):
                out_re[chunk, cut] = g_out[:, chunk * 128 : (chunk + 1) * 128]
                out_im[chunk, cut] = h_out[:, chunk * 128 : (chunk + 1) * 128]

        for k in range(GROUP):
            p = step * GROUP + k
            i = pairs[base + p, 0]
            j = pairs[base + p, 1]
            at = k * 4 * local
            for chunk in range(freq // 128):
                cut = pl.ds(chunk * 128, 128)
                to_second = [None] * (4 * local)
                to_first = [None] * (4 * local)
                add = lambda total, term: term if total is None else total + term
                for c in range(part):
                    g = out_re[chunk, pl.ds(k * rows + c * part, part)]
                    h = out_im[chunk, pl.ds(k * rows + c * part, part)]
                    for w in range(2 * local):
                        a = first[at + 2 * w, pl.ds(c, 1), cut]
                        b = first[at + 2 * w + 1, pl.ds(c, 1), cut]
                        to_second[2 * w] = add(to_second[2 * w], g * a - h * b)
                        to_second[2 * w + 1] = add(to_second[2 * w + 1], g * b + h * a)
                for w in range(2 * local):
                    target = own_grad if w < local else other_grad
                    for c in range(2):
                        target[j, w % local, c, pl.ds(second_part * part, part), cut] += to_second[2 * w + c]
                for c in range(part):
                    g = out_re[chunk, pl.ds(k * rows + c, part, stride=part)]
                    h = out_im[chunk, pl.ds(k * rows + c, part, stride=part)]
                    for w in range(2 * local):
                        a = second[at + 2 * w, pl.ds(c, 1), cut]
                        b = second[at + 2 * w + 1, pl.ds(c, 1), cut]
                        to_first[2 * w] = add(to_first[2 * w], g * a + h * b)
                        to_first[2 * w + 1] = add(to_first[2 * w + 1], g * b - h * a)
                for w in range(2 * local):
                    target = own_grad if w < local else other_grad
                    for c in range(2):
                        target[i, w % local, c, pl.ds(first_part * part, part), cut] += to_first[2 * w + c]
        return carry

    lax.fori_loop(0, pair_count // GROUP, work, 0)


def team_kernel(meta, pairs, mask, *refs):
    count = len(HOPS[0])
    came, refs = refs[: 2 * count], refs[2 * count :]
    (
        cos_hbm,
        sin_hbm,
        alternate,
        weight,
        keep,
        give,
        misfit,
        field,
        grad,
        cross_re,
        cross_im,
        plus_adj,
        minus_adj,
        edge_adj,
        out_re,
        out_im,
        cos,
        sin,
        sems,
    ) = refs
    copies = [
        pltpu.make_async_copy(cos_hbm, cos, sems.at[0]),
        pltpu.make_async_copy(sin_hbm, sin, sems.at[1]),
    ]
    for copy in copies:
        copy.start()
    pair_count = misfit.shape[0]
    windows = field.shape[1]
    chunks, part = field.shape[4:6]
    freq = chunks * 128
    rows = part * part
    wide = 256
    steps = pair_count // GROUP
    first_part = meta[1]
    second_part = meta[2]
    lane = lax.broadcasted_iota(jnp.int32, (rows, 128), 1)

    for n, parcel in enumerate(came):
        index = meta[4 + n]
        for w in range(windows):
            m = mask[w, index].astype(jnp.float32)
            for c in range(2):
                both = parcel[w, c].astype(jnp.float32) * m
                for half in range(2):
                    for chunk in range(chunks):
                        field[index, w, c, half, chunk] = both[
                            half * part : (half + 1) * part, chunk * 128 : (chunk + 1) * 128
                        ]
    grad[...] = jnp.zeros_like(grad)

    def row_of(index, w, c, half, chunk, row):
        return field[index, w, c, half, chunk, pl.ds(row, 1)]

    def scale_of(p, factor):
        i = pairs[p, 0]
        j = pairs[p, 1]
        shared = jnp.int32(0)
        for w in range(windows):
            shared = shared + mask[w, i] * mask[w, j]
        shared = jnp.maximum(shared, 1).astype(jnp.float32) * (2.0 * freq * factor)
        return lax.rsqrt(jnp.full((1, 128), shared, jnp.float32))

    def cross(s, k):
        p = s * GROUP + k
        i = pairs[p, 0]
        j = pairs[p, 1]
        for chunk in range(chunks):
            to = slice(chunk * 128, (chunk + 1) * 128)
            right = [
                [field[j, w, c, second_part, chunk] for c in range(2)] for w in range(windows)
            ]
            for row in range(0, part, 2):
                found = []
                for c1 in (row, row + 1):
                    re = im = None
                    for w in range(windows):
                        a = row_of(i, w, 0, first_part, chunk, c1)
                        b = row_of(i, w, 1, first_part, chunk, c1)
                        aa = a * right[w][0] + b * right[w][1]
                        ab = a * right[w][1] - b * right[w][0]
                        re = aa if re is None else re + aa
                        im = ab if im is None else im + ab
                    found.append((re, im))
                at = slice(k * rows + row * part, k * rows + (row + 2) * part)
                for target, n in ((cross_re, 0), (cross_im, 1)):
                    both = jnp.concatenate([found[0][n], found[1][n]], axis=0)
                    target[s % 2, at, to] = both.astype(jnp.bfloat16)

    def forward(s, n):
        cut = slice(n * wide, (n + 1) * wide)
        even = jnp.dot(cross_re[s % 2], cos[:, cut], preferred_element_type=jnp.float32)
        odd = jnp.dot(cross_im[s % 2], sin[:, cut], preferred_element_type=jnp.float32)
        return even, odd

    def forward_edge(s):
        return jnp.dot(cross_re[s % 2], alternate[...], preferred_element_type=jnp.float32)

    def shape_edge(s, edge, totals):
        for k in range(GROUP):
            at = slice(k * rows, (k + 1) * rows)
            value = edge[at] * (0.5 * scale_of(s * GROUP + k, 1.0))
            source = value * value * value * 0.125
            edge_adj[s % 2, at] = source.astype(jnp.bfloat16).astype(jnp.float32)
            totals[k] = jnp.where(lane == 0, source * value, 0.0)

    def shape(s, n, sums, totals):
        for k in range(GROUP):
            at = slice(k * rows, (k + 1) * rows)
            scale = 0.5 * scale_of(s * GROUP + k, 1.0)
            for chunk in range(wide // 128):
                cut = slice(chunk * 128, (chunk + 1) * 128)
                to = slice(n * wide + chunk * 128, n * wide + (chunk + 1) * 128)
                even = sums[0][at, cut] * scale
                odd = sums[1][at, cut] * (3.0 * scale)
                plus = even + odd
                minus = even - odd
                if n == 0 and chunk == 0:
                    minus = jnp.where(lane == 0, 0.0, minus)
                plus_source = plus * plus * plus * weight[0:1, to]
                minus_source = minus * minus * minus * weight[1:2, to]
                plus_adj[s % 2, at, to] = plus_source.astype(jnp.bfloat16)
                minus_adj[s % 2, at, to] = minus_source.astype(jnp.bfloat16)
                totals[k] = totals[k] + (plus_source * plus + minus_source * minus)

    def tell(s, totals):
        for k in range(GROUP):
            p = s * GROUP + k
            misfit[p : p + 1] = jnp.sum(totals[k], axis=0, keepdims=True)

    def back(s, n, which):
        cut = slice(n * wide, (n + 1) * wide)
        table = sin if which else cos
        up = jnp.dot(plus_adj[s % 2], table[:, cut], preferred_element_type=jnp.float32)
        down = jnp.dot(minus_adj[s % 2], table[:, cut], preferred_element_type=jnp.float32)
        return up, down

    def scale_back(s, n, which, sums):
        sign = 1.0 - 2.0 * (lane % 2).astype(jnp.float32)
        for k in range(GROUP):
            at = slice(k * rows, (k + 1) * rows)
            scale = scale_of(s * GROUP + k, 4.0 * part)
            extra = None if which else edge_adj[s % 2, at] * sign
            for chunk in range(wide // 128):
                cut = slice(chunk * 128, (chunk + 1) * 128)
                if which:
                    value = sums[0][at, cut] - sums[1][at, cut]
                else:
                    value = sums[0][at, cut] + sums[1][at, cut] + extra
                value = (value * scale).astype(jnp.bfloat16).astype(jnp.float32)
                target = out_im if which else out_re
                target[s % 2, n * (wide // 128) + chunk, at] = value

    def gradient(s, k):
        p = s * GROUP + k
        i = pairs[p, 0]
        j = pairs[p, 1]
        add = lambda total, term: term if total is None else total + term
        for chunk in range(chunks):
            for toward_first in (False, True):
                sums = [[None, None] for w in range(windows)]
                for c in range(part):
                    if toward_first:
                        at = pl.ds(k * rows + c, part, stride=part)
                    else:
                        at = pl.ds(k * rows + c * part, part)
                    g = out_re[s % 2, chunk, at]
                    h = out_im[s % 2, chunk, at]
                    for w in range(windows):
                        if toward_first:
                            a = row_of(j, w, 0, second_part, chunk, c)
                            b = row_of(j, w, 1, second_part, chunk, c)
                            re, im = g * a + h * b, g * b - h * a
                        else:
                            a = row_of(i, w, 0, first_part, chunk, c)
                            b = row_of(i, w, 1, first_part, chunk, c)
                            re, im = g * a - h * b, g * b + h * a
                        sums[w] = [add(sums[w][0], re), add(sums[w][1], im)]
                index = i if toward_first else j
                half = first_part if toward_first else second_part
                for w in range(windows):
                    for c in range(2):
                        grad[index, w, c, half, chunk] += sums[w][c]

    def start(s, fill):
        totals = [None] * GROUP
        edge = forward_edge(s)
        found = [forward(s, 0)]
        fill = list(fill)
        for call in fill[: len(fill) // 2]:
            call()
        shape_edge(s, edge, totals)
        for n in range(1, freq // wide):
            found.append(forward(s, n))
            shape(s, n - 1, found[n - 1], totals)
        for call in fill[len(fill) // 2 :]:
            call()
        shape(s, freq // wide - 1, found[-1], totals)
        tell(s, totals)

    for k in range(GROUP):
        cross(0, k)
    for copy in copies:
        copy.wait()
    start(0, [])
    for s in range(steps):
        fill = []
        late = []
        for k in range(GROUP):
            if s + 1 < steps:
                fill.append(functools.partial(cross, s + 1, k))
            if s > 0:
                (fill if k < GROUP // 2 or s + 1 == steps else late).append(
                    functools.partial(gradient, s - 1, k)
                )
        pieces = [(n, which) for n in range(freq // wide) for which in range(2)]
        share = -(-len(fill) // len(pieces))
        for m, (n, which) in enumerate(pieces):
            sums = back(s, n, which)
            for call in fill[m * share : (m + 1) * share]:
                call()
            scale_back(s, n, which, sums)
        if s + 1 < steps:
            start(s + 1, late)
    for k in range(GROUP):
        gradient(steps - 1, k)

    size = 2 * part
    for n in range(2 * count):
        index = meta[4 + n]
        target = keep if n < count else give
        for w in range(windows):
            m = mask[w, index].astype(jnp.float32)
            for c in range(2):
                at = (((n % count) * windows + w) * 2 + c) * size
                for chunk in range(chunks):
                    term = jnp.concatenate(
                        [grad[index, w, c, half, chunk] for half in range(2)], axis=0
                    )
                    to = slice(chunk * 128, (chunk + 1) * 128)
                    target[at : at + size, to] = (term * m).astype(target.dtype)
    give[count * windows * 2 * size :] = note_of(misfit[...], pair_count // 2)


def per_device(spectra, block_pairs, owners, window_mask):
    blk_count = lax.axis_size("blk")
    blk_index = lax.axis_index("blk")
    core = lax.axis_index("win")
    local = spectra.shape[0]
    channels = spectra.shape[3]
    freq = spectra.shape[4]
    part = channels // PARTS
    pair_total = block_pairs.shape[0]
    teams = blk_count // TEAM
    pair_count = pair_total // teams
    direct = teams == 1
    swap = [(0, 1), (1, 0)]
    smem = pl.BlockSpec(memory_space=pltpu.SMEM)
    vmem = pl.BlockSpec(memory_space=pltpu.VMEM)
    hbm = pl.BlockSpec(memory_space=pltpu.HBM)
    small = pltpu.CompilerParams(vmem_limit_bytes=SMALL_VMEM)
    count = len(HOPS[0])
    hop_pairs = [
        [(2 * b + c, 2 * (b ^ HOPS[c][r]) + c) for b in range(TEAM) for c in range(2)]
        for r in range(count)
    ]
    rank = blk_index if direct else lax.rem(blk_index, TEAM)
    meta = lax.dynamic_slice_in_dim(jnp.asarray(positions()), rank * 2 + core, 1)[0]
    if not direct:
        meta = meta.at[0].set(lax.div(blk_index, TEAM) * pair_count)

    owner_ids = owners[:, 0]
    order = jnp.arange(pair_total, dtype=jnp.int32)
    earlier = (owner_ids[:, None] == owner_ids[None, :]) & (order[None, :] < order[:, None])
    slot = owner_ids * CAP + jnp.sum(earlier.astype(jnp.int32), axis=1)
    mine_slots = blk_index * CAP + jnp.arange(CAP, dtype=jnp.int32)
    chosen = (slot[:, None] == mine_slots[None, :]).astype(jnp.float32)
    misfit_scale = 1.0 / (channels * channels * 2.0 * freq)

    if direct:
        other = lax.ppermute(spectra, "win", swap)
        parcel_type = jax.ShapeDtypeStruct((2 * local, 2, 2 * part, freq), jnp.bfloat16)
        parcels = pl.pallas_call(
            pack_kernel,
            out_shape=(parcel_type,) * count,
            in_specs=[smem, vmem, vmem],
            out_specs=(vmem,) * count,
            scratch_shapes=[pltpu.VMEM((PARTS, part, freq), jnp.float32)],
            compiler_params=small,
        )(meta, spectra, other)
        landed = [
            lax.ppermute(parcel, ("blk", "win"), pairs) for parcel, pairs in zip(parcels, hop_pairs)
        ]
        came = landed + [lax.ppermute(parcel, "win", swap) for parcel in landed]
    else:
        pieces = spectra[:, 0].reshape(local, 2, PARTS, part, freq)
        outgoing = jnp.stack(
            [jnp.stack([pieces[:, :, s] for s in SUBSETS[r]], axis=2) for r in range(TEAM)]
        ).reshape(TEAM, local, 2, 2 * part, freq)
        outgoing = jnp.tile(outgoing, (teams, 1, 1, 1, 1))
        own = lax.all_to_all(outgoing, "blk", split_axis=0, concat_axis=0, tiled=True)
        came = [own, lax.ppermute(own, "win", swap)]

    rows = part * part * GROUP
    parcel_rows = 2 * local * 2 * 2 * part
    misfit_type = jax.ShapeDtypeStruct((pair_count, 128), jnp.float32)
    if direct:
        split_shape = (blk_count, 2 * local, 2, 2, freq // 128, part, 128)
        keep, give, misfit = pl.pallas_call(
            team_kernel,
            out_shape=(
                jax.ShapeDtypeStruct((count * parcel_rows, freq), jnp.float32),
                jax.ShapeDtypeStruct((count * parcel_rows + pair_count // 2, freq), jnp.bfloat16),
                misfit_type,
            ),
            in_specs=[smem] * 3 + [vmem] * len(came) + [hbm] * 2 + [vmem] * 2,
            out_specs=(vmem, vmem, vmem),
            scratch_shapes=[
                pltpu.VMEM(split_shape, jnp.float32),
                pltpu.VMEM(split_shape, jnp.float32),
                pltpu.VMEM((2, rows, freq), jnp.bfloat16),
                pltpu.VMEM((2, rows, freq), jnp.bfloat16),
                pltpu.VMEM((2, rows, freq), jnp.bfloat16),
                pltpu.VMEM((2, rows, freq), jnp.bfloat16),
                pltpu.VMEM((2, rows, 128), jnp.float32),
                pltpu.VMEM((2, freq // 128, rows, 128), jnp.float32),
                pltpu.VMEM((2, freq // 128, rows, 128), jnp.float32),
                pltpu.VMEM((freq, freq), jnp.bfloat16),
                pltpu.VMEM((freq, freq), jnp.bfloat16),
                pltpu.SemaphoreType.DMA((2,)),
            ],
            compiler_params=pltpu.CompilerParams(vmem_limit_bytes=24 << 20),
        )(meta, block_pairs, window_mask, *came, *team_tables(freq))
        swapped = lax.ppermute(give, "win", swap)
        parcel_type = jax.ShapeDtypeStruct((parcel_rows + pair_count // 2, freq), jnp.bfloat16)
        parcels = pl.pallas_call(
            add_kernel,
            out_shape=(parcel_type,) * count,
            in_specs=[vmem] * 3,
            out_specs=(vmem,) * count,
            compiler_params=small,
        )(keep, swapped, misfit)
        landed = [
            lax.ppermute(parcel, ("blk", "win"), pairs) for parcel, pairs in zip(parcels, hop_pairs)
        ]
        half_type = jax.ShapeDtypeStruct((local * 2 * channels + pair_count, freq), jnp.float32)
        mine, give = pl.pallas_call(
            merge_kernel,
            out_shape=(half_type, half_type),
            in_specs=[smem] + [vmem] * count,
            out_specs=(vmem, vmem),
            scratch_shapes=[pltpu.VMEM((2 * local, 2, PARTS, part, freq), jnp.float32)],
            compiler_params=small,
        )(meta, *landed)
        swapped = lax.ppermute(give, "win", swap)
        gradient, totals = pl.pallas_call(
            functools.partial(finish_kernel, scale=misfit_scale),
            out_shape=(
                jax.ShapeDtypeStruct(spectra.shape, jnp.bfloat16),
                jax.ShapeDtypeStruct((1, CAP), jnp.float32),
            ),
            in_specs=[vmem] * 3,
            out_specs=(vmem, vmem),
            compiler_params=small,
        )(mine, swapped, chosen)
        return (gradient, totals.reshape(CAP))
    half = jax.ShapeDtypeStruct((blk_count, local, 2, 2 * part, freq), jnp.float32)
    own_grad, other_grad, misfit = pl.pallas_call(
        pair_kernel,
        out_shape=(half, half, jax.ShapeDtypeStruct((pair_count, freq), jnp.float32)),
        in_specs=[smem] * 3 + [vmem] * 7,
        out_specs=(vmem, vmem, vmem),
        scratch_shapes=[
            pltpu.VMEM((GROUP * 4 * local, part, freq), jnp.float32),
            pltpu.VMEM((GROUP * 4 * local, part, freq), jnp.float32),
            pltpu.VMEM((rows, freq), jnp.bfloat16),
            pltpu.VMEM((rows, freq), jnp.bfloat16),
            pltpu.VMEM((rows, 2 * freq), jnp.bfloat16),
            pltpu.VMEM((freq // 128, rows, 128), jnp.float32),
            pltpu.VMEM((freq // 128, rows, 128), jnp.float32),
        ],
        compiler_params=pltpu.CompilerParams(
            vmem_limit_bytes=(16 << 20) + 3 * math.prod(half.shape) * 4
        ),
    )(meta, block_pairs, window_mask, *came, *tables(freq))

    swapped = lax.ppermute(other_grad.astype(jnp.bfloat16), "win", swap)
    terms = jnp.sum(misfit, axis=1)
    terms = terms + lax.ppermute(terms, "win", swap)
    chip_grad = (own_grad + swapped.astype(jnp.float32)).astype(jnp.bfloat16)
    high = terms.astype(jnp.bfloat16)
    low = (terms - high.astype(jnp.float32)).astype(jnp.bfloat16)
    note = jnp.zeros((8, freq), jnp.bfloat16).at[0, :pair_count].set(high).at[1, :pair_count].set(low)
    grad_rows = local * 2 * 2 * part
    payload = jnp.concatenate(
        [
            chip_grad.reshape(blk_count, grad_rows, freq),
            jnp.broadcast_to(note[None], (blk_count, 8, freq)),
        ],
        axis=1,
    )
    arrived = lax.all_to_all(payload, "blk", split_axis=0, concat_axis=0, tiled=True)
    wide = arrived[:, :grad_rows].reshape(teams, TEAM, local, 2, 2, part, freq).astype(jnp.float32)
    wide = jnp.sum(wide, axis=0)
    gradient = jnp.stack(
        [
            sum(wide[r, :, :, SUBSETS[r].index(s)] for r in range(TEAM) if s in SUBSETS[r])
            for s in range(PARTS)
        ],
        axis=2,
    )
    gradient = gradient.reshape(local, 1, 2, channels, freq).astype(jnp.bfloat16)
    notes = arrived[:, grad_rows:, :pair_count].astype(jnp.float32)
    notes = jnp.sum((notes[:, 0] + notes[:, 1]).reshape(teams, TEAM, pair_count), axis=1)
    pair_misfit = notes.reshape(pair_total) * misfit_scale
    totals = jnp.sum(pair_misfit[:, None] * chosen, axis=0)
    return (gradient, totals)


def solution(mesh):
    return jax.shard_map(
        per_device,
        mesh=mesh,
        in_specs=(
            P("win", ("groups", "blk"), None, None, None),
            P("groups", None),
            P("groups", None),
            P(None, "groups"),
        ),
        out_specs=(P("win", ("groups", "blk"), None, None, None), P(("groups", "blk"))),
        check_vma=False,
    )
```

```python
import functools
import math

import jax
import jax.numpy as jnp
import ml_dtypes
import numpy as np
from jax import lax
from jax.experimental import pallas as pl
from jax.experimental.pallas import tpu as pltpu
from jax.sharding import PartitionSpec as P

CAP = 3
PARTS = 4
TEAM = 8
SUBSETS = ((0, 1), (0, 1), (0, 2), (0, 3), (1, 2), (1, 3), (2, 3), (2, 3))
GROUP = 4
SMALL_VMEM = 6 << 20
HOPS = ((6, 4, 2, 0), (7, 5, 3, 1))


@functools.lru_cache(maxsize=None)
def tables(freq_count):
    lag_count = 2 * freq_count
    f = np.arange(freq_count)[:, None]
    t = np.arange(freq_count)[None, :]
    phase = (f * t % lag_count) * (2.0 * np.pi / lag_count)
    cos = np.cos(phase)
    sin = -np.sin(phase)
    alternate = np.where(np.arange(freq_count) % 2 == 0, 1.0, -1.0)
    extra = np.zeros((freq_count, 128))
    extra[:, 0] = alternate
    forward_re = np.concatenate([cos, extra], axis=1)
    cos_back = cos.T
    cos_mirror = cos_back.copy()
    cos_mirror[0] = alternate
    back_re = np.concatenate([cos_back, cos_mirror], axis=0)
    back_im = np.concatenate([sin.T, -sin.T], axis=0)
    taper = 1.0 + np.cos(np.pi * np.arange(lag_count) / lag_count)
    mirror = np.concatenate([[freq_count], lag_count - np.arange(1, freq_count)])
    weight = np.stack([taper[:freq_count], taper[mirror]]) / 8.0
    as_bf16 = lambda x: x.astype(np.float32).astype(ml_dtypes.bfloat16)
    return (
        as_bf16(forward_re),
        as_bf16(sin),
        as_bf16(back_re),
        as_bf16(back_im),
        weight.astype(np.float32),
    )


@functools.lru_cache(maxsize=None)
def positions():
    out = np.zeros((TEAM, 2, 28), np.int32)
    for rank in range(TEAM):
        for core in range(2):
            same = rank in (0, TEAM - 1)
            row = [0, core, core if same else 1 - core, core]
            row += [rank ^ hop for hop in HOPS[core]]
            row += [rank ^ hop for hop in HOPS[1 - core]]
            for hop in HOPS[core] + HOPS[1 - core]:
                row += SUBSETS[rank ^ hop]
            out[rank, core] = row
    return out.reshape(TEAM * 2, -1)


def team_tables(freq_count):
    forward_re, forward_im, _, _, weight = tables(freq_count)
    turn = np.broadcast_to(forward_re[:, freq_count : freq_count + 1], (freq_count, 128))
    in_hbm = [
        pltpu.with_memory_space_constraint(jnp.asarray(table), pltpu.HBM)
        for table in (forward_re[:, :freq_count], forward_im)
    ]
    return (*in_hbm, jnp.asarray(turn), jnp.asarray(weight))


def pack_kernel(meta, own, other, *refs):
    parcels, wide = refs[:-1], refs[-1]
    local = own.shape[0]
    core = meta[3]
    for source, side in ((own, core), (other, 1 - core)):
        for w in range(local):
            for c in range(2):
                wide[...] = source[w, 0, c].astype(jnp.float32).reshape(wide.shape)
                for r, parcel in enumerate(parcels):
                    both = [wide[meta[12 + 2 * r + n]] for n in range(2)]
                    parcel[side * local + w, c] = jnp.concatenate(both, axis=0).astype(jnp.bfloat16)


def add_kernel(keep, came, terms, *parcels):
    count = len(parcels)
    rows = keep.shape[0] // count
    pair_count = terms.shape[0]
    half = pair_count // 2
    arrived = came[count * rows :].astype(jnp.float32)
    total = terms[...] + jnp.concatenate(
        [arrived[:, :128] + arrived[:, 256:384], arrived[:, 128:256] + arrived[:, 384:512]], axis=0
    )
    note = note_of(total, half)
    for r, parcel in enumerate(parcels):
        cut = slice(r * rows, (r + 1) * rows)
        parcel[:rows] = (keep[cut] + came[cut].astype(jnp.float32)).astype(jnp.bfloat16)
        parcel[rows:] = note


def note_of(total, half):
    high = total.astype(jnp.bfloat16).astype(jnp.float32)
    low = total - high
    return jnp.concatenate([high[:half], high[half:], low[:half], low[half:]], axis=1).astype(
        jnp.bfloat16
    )


def merge_kernel(meta, *refs, scale):
    parcels, (chosen, gradient, totals, total) = refs[:-4], refs[-4:]
    local, _, _, part, freq = total.shape
    core = meta[3]
    size = 2 * part
    rows = 4 * local * size
    note = None
    total[...] = jnp.zeros_like(total)
    for n, parcel in enumerate(parcels):
        for w in range(local):
            for c in range(2):
                start = pl.multiple_of(((core * local + w) * 2 + c) * size, size)
                both = parcel[pl.ds(start, size)].astype(jnp.float32)
                for half in range(2):
                    at = slice(half * part, (half + 1) * part)
                    total[w, c, meta[12 + 2 * n + half]] += both[at]
        tail = parcel[rows:].astype(jnp.float32)
        tail = jnp.concatenate(
            [tail[:, :128] + tail[:, 256:384], tail[:, 128:256] + tail[:, 384:512]], axis=0
        )
        note = tail if note is None else note + tail
    for w in range(local):
        for c in range(2):
            gradient[w, 0, c] = total[w, c].reshape(PARTS * part, freq).astype(jnp.bfloat16)
    pair = jnp.sum(note, axis=1, keepdims=True) * scale
    totals[...] = jnp.sum(pair * chosen[...], axis=0, keepdims=True)


def pair_kernel(
    meta,
    pairs,
    mask,
    own,
    other,
    forward_re,
    forward_im,
    back_re,
    back_im,
    weight,
    own_grad,
    other_grad,
    misfit,
    first,
    second,
    cross_re,
    cross_im,
    adj,
    out_re,
    out_im,
):
    pair_count = misfit.shape[0]
    freq = own.shape[-1]
    part = own.shape[3] // 2
    local = own.shape[1]
    base = meta[0]
    first_part = meta[1]
    second_part = meta[2]
    core = meta[3]
    rows = part * part
    lanes = 256

    own_grad[...] = jnp.zeros_like(own_grad)
    other_grad[...] = jnp.zeros_like(other_grad)

    def block(source, index, w, c, which):
        both = source[index, w, c].astype(jnp.float32)
        return jnp.where(which == 0, both[:part], both[part:])

    def work(step, carry):
        counts = []
        for k in range(GROUP):
            p = step * GROUP + k
            i = pairs[base + p, 0]
            j = pairs[base + p, 1]
            shared = jnp.int32(0)
            for w in range(2 * local):
                is_own = w < local
                source = own if is_own else other
                side = core if is_own else 1 - core
                where = side * local + w % local
                m = mask[where, i] * mask[where, j]
                shared = shared + m
                m = m.astype(jnp.float32)
                for c in range(2):
                    at = k * 4 * local + w * 2 + c
                    first[at] = block(source, i, w % local, c, first_part) * m
                    second[at] = block(source, j, w % local, c, second_part) * m
            counts.append(jnp.maximum(shared, 1).astype(jnp.float32) * (2.0 * freq))
            for chunk in range(freq // lanes):
                cut = pl.ds(chunk * lanes, lanes)
                right = [second[k * 4 * local + n, :, cut] for n in range(4 * local)]
                for c1 in range(part):
                    re = None
                    for w in range(2 * local):
                        a = first[k * 4 * local + 2 * w, pl.ds(c1, 1), cut]
                        b = first[k * 4 * local + 2 * w + 1, pl.ds(c1, 1), cut]
                        aa = a * right[2 * w] + b * right[2 * w + 1]
                        ab = a * right[2 * w + 1] - b * right[2 * w]
                        re = aa if re is None else re + aa
                        im = ab if w == 0 else im + ab
                    cross_re[pl.ds(k * rows + c1 * part, part), cut] = re.astype(jnp.bfloat16)
                    cross_im[pl.ds(k * rows + c1 * part, part), cut] = im.astype(jnp.bfloat16)

        cos_sum = jnp.dot(cross_re[...], forward_re[...], preferred_element_type=jnp.float32)
        sin_sum = jnp.dot(cross_im[...], forward_im[...], preferred_element_type=jnp.float32)
        lane = lax.broadcasted_iota(jnp.int32, (rows, freq), 1)
        for k in range(GROUP):
            cut = slice(k * rows, (k + 1) * rows)
            scale = 0.5 * lax.rsqrt(jnp.full((1, freq), counts[k], jnp.float32))
            even = cos_sum[cut, :freq] * scale
            odd = sin_sum[cut] * (3.0 * scale)
            middle = cos_sum[cut, freq : freq + 1] * scale
            plus = even + odd
            minus = jnp.where(lane == 0, middle, even - odd)
            plus_adj = plus * plus * plus * weight[0:1, :]
            minus_adj = minus * minus * minus * weight[1:2, :]
            adj[cut, :freq] = plus_adj.astype(jnp.bfloat16)
            adj[cut, freq:] = minus_adj.astype(jnp.bfloat16)
            total = plus_adj * plus + minus_adj * minus
            misfit[pl.ds(step * GROUP + k, 1), :] = jnp.sum(total, axis=0, keepdims=True)
        g_sum = jnp.dot(adj[...], back_re[...], preferred_element_type=jnp.float32)
        h_sum = jnp.dot(adj[...], back_im[...], preferred_element_type=jnp.float32)
        for k in range(GROUP):
            cut = slice(k * rows, (k + 1) * rows)
            scale = lax.rsqrt(jnp.full((1, freq), counts[k] * (4.0 * part), jnp.float32))
            g_out = (g_sum[cut] * scale).astype(jnp.bfloat16).astype(jnp.float32)
            h_out = (h_sum[cut] * scale).astype(jnp.bfloat16).astype(jnp.float32)
            for chunk in range(freq // 128):
                out_re[chunk, cut] = g_out[:, chunk * 128 : (chunk + 1) * 128]
                out_im[chunk, cut] = h_out[:, chunk * 128 : (chunk + 1) * 128]

        for k in range(GROUP):
            p = step * GROUP + k
            i = pairs[base + p, 0]
            j = pairs[base + p, 1]
            at = k * 4 * local
            for chunk in range(freq // 128):
                cut = pl.ds(chunk * 128, 128)
                to_second = [None] * (4 * local)
                to_first = [None] * (4 * local)
                add = lambda total, term: term if total is None else total + term
                for c in range(part):
                    g = out_re[chunk, pl.ds(k * rows + c * part, part)]
                    h = out_im[chunk, pl.ds(k * rows + c * part, part)]
                    for w in range(2 * local):
                        a = first[at + 2 * w, pl.ds(c, 1), cut]
                        b = first[at + 2 * w + 1, pl.ds(c, 1), cut]
                        to_second[2 * w] = add(to_second[2 * w], g * a - h * b)
                        to_second[2 * w + 1] = add(to_second[2 * w + 1], g * b + h * a)
                for w in range(2 * local):
                    target = own_grad if w < local else other_grad
                    for c in range(2):
                        target[j, w % local, c, pl.ds(second_part * part, part), cut] += to_second[2 * w + c]
                for c in range(part):
                    g = out_re[chunk, pl.ds(k * rows + c, part, stride=part)]
                    h = out_im[chunk, pl.ds(k * rows + c, part, stride=part)]
                    for w in range(2 * local):
                        a = second[at + 2 * w, pl.ds(c, 1), cut]
                        b = second[at + 2 * w + 1, pl.ds(c, 1), cut]
                        to_first[2 * w] = add(to_first[2 * w], g * a + h * b)
                        to_first[2 * w + 1] = add(to_first[2 * w + 1], g * b - h * a)
                for w in range(2 * local):
                    target = own_grad if w < local else other_grad
                    for c in range(2):
                        target[i, w % local, c, pl.ds(first_part * part, part), cut] += to_first[2 * w + c]
        return carry

    lax.fori_loop(0, pair_count // GROUP, work, 0)


def team_kernel(meta, pairs, mask, *refs):
    count = len(HOPS[0])
    came, refs = refs[: 2 * count], refs[2 * count :]
    (
        cos_hbm,
        sin_hbm,
        alternate,
        weight,
        keep,
        give,
        misfit,
        field,
        grad,
        cross_re,
        cross_im,
        plus_adj,
        minus_adj,
        edge_adj,
        out_re,
        out_im,
        cos,
        sin,
        sems,
    ) = refs
    copies = [
        pltpu.make_async_copy(cos_hbm, cos, sems.at[0]),
        pltpu.make_async_copy(sin_hbm, sin, sems.at[1]),
    ]
    for copy in copies:
        copy.start()
    pair_count = misfit.shape[0]
    windows = field.shape[1]
    chunks, part = field.shape[4:6]
    freq = chunks * 128
    rows = part * part
    wide = 256
    steps = pair_count // GROUP
    first_part = meta[1]
    second_part = meta[2]
    lane = lax.broadcasted_iota(jnp.int32, (rows, 128), 1)

    for n, parcel in enumerate(came):
        index = meta[4 + n]
        for w in range(windows):
            m = mask[w, index].astype(jnp.float32)
            for c in range(2):
                both = parcel[w, c].astype(jnp.float32) * m
                for half in range(2):
                    for chunk in range(chunks):
                        field[index, w, c, half, chunk] = both[
                            half * part : (half + 1) * part, chunk * 128 : (chunk + 1) * 128
                        ]
    grad[...] = jnp.zeros_like(grad)

    def row_of(index, w, c, half, chunk, row):
        return field[index, w, c, half, chunk, pl.ds(row, 1)]

    def scale_of(p, factor):
        i = pairs[p, 0]
        j = pairs[p, 1]
        shared = jnp.int32(0)
        for w in range(windows):
            shared = shared + mask[w, i] * mask[w, j]
        shared = jnp.maximum(shared, 1).astype(jnp.float32) * (2.0 * freq * factor)
        return lax.rsqrt(jnp.full((1, 128), shared, jnp.float32))

    def cross(s, k):
        p = s * GROUP + k
        i = pairs[p, 0]
        j = pairs[p, 1]
        for chunk in range(chunks):
            to = slice(chunk * 128, (chunk + 1) * 128)
            right = [
                [field[j, w, c, second_part, chunk] for c in range(2)] for w in range(windows)
            ]
            for row in range(0, part, 2):
                found = []
                for c1 in (row, row + 1):
                    re = im = None
                    for w in range(windows):
                        a = row_of(i, w, 0, first_part, chunk, c1)
                        b = row_of(i, w, 1, first_part, chunk, c1)
                        aa = a * right[w][0] + b * right[w][1]
                        ab = a * right[w][1] - b * right[w][0]
                        re = aa if re is None else re + aa
                        im = ab if im is None else im + ab
                    found.append((re, im))
                at = slice(k * rows + row * part, k * rows + (row + 2) * part)
                for target, n in ((cross_re, 0), (cross_im, 1)):
                    both = jnp.concatenate([found[0][n], found[1][n]], axis=0)
                    target[s % 2, at, to] = both.astype(jnp.bfloat16)

    def forward(s, n):
        cut = slice(n * wide, (n + 1) * wide)
        even = jnp.dot(cross_re[s % 2], cos[:, cut], preferred_element_type=jnp.float32)
        odd = jnp.dot(cross_im[s % 2], sin[:, cut], preferred_element_type=jnp.float32)
        return even, odd

    def forward_edge(s):
        return jnp.dot(cross_re[s % 2], alternate[...], preferred_element_type=jnp.float32)

    def shape_edge(s, edge, totals):
        for k in range(GROUP):
            at = slice(k * rows, (k + 1) * rows)
            value = edge[at] * (0.5 * scale_of(s * GROUP + k, 1.0))
            source = value * value * value * 0.125
            edge_adj[s % 2, at] = source.astype(jnp.bfloat16).astype(jnp.float32)
            totals[k] = jnp.where(lane == 0, source * value, 0.0)

    def shape(s, n, sums, totals):
        for k in range(GROUP):
            at = slice(k * rows, (k + 1) * rows)
            scale = 0.5 * scale_of(s * GROUP + k, 1.0)
            for chunk in range(wide // 128):
                cut = slice(chunk * 128, (chunk + 1) * 128)
                to = slice(n * wide + chunk * 128, n * wide + (chunk + 1) * 128)
                even = sums[0][at, cut] * scale
                odd = sums[1][at, cut] * (3.0 * scale)
                plus = even + odd
                minus = even - odd
                if n == 0 and chunk == 0:
                    minus = jnp.where(lane == 0, 0.0, minus)
                plus_source = plus * plus * plus * weight[0:1, to]
                minus_source = minus * minus * minus * weight[1:2, to]
                plus_adj[s % 2, at, to] = plus_source.astype(jnp.bfloat16)
                minus_adj[s % 2, at, to] = minus_source.astype(jnp.bfloat16)
                totals[k] = totals[k] + (plus_source * plus + minus_source * minus)

    def tell(s, totals):
        for k in range(GROUP):
            p = s * GROUP + k
            misfit[p : p + 1] = jnp.sum(totals[k], axis=0, keepdims=True)

    def back(s, n, which):
        cut = slice(n * wide, (n + 1) * wide)
        table = sin if which else cos
        up = jnp.dot(plus_adj[s % 2], table[:, cut], preferred_element_type=jnp.float32)
        down = jnp.dot(minus_adj[s % 2], table[:, cut], preferred_element_type=jnp.float32)
        return up, down

    def scale_back(s, n, which, sums):
        sign = 1.0 - 2.0 * (lane % 2).astype(jnp.float32)
        for k in range(GROUP):
            at = slice(k * rows, (k + 1) * rows)
            scale = scale_of(s * GROUP + k, 4.0 * part)
            extra = None if which else edge_adj[s % 2, at] * sign
            for chunk in range(wide // 128):
                cut = slice(chunk * 128, (chunk + 1) * 128)
                if which:
                    value = sums[0][at, cut] - sums[1][at, cut]
                else:
                    value = sums[0][at, cut] + sums[1][at, cut] + extra
                value = (value * scale).astype(jnp.bfloat16).astype(jnp.float32)
                target = out_im if which else out_re
                target[s % 2, n * (wide // 128) + chunk, at] = value

    def gradient(s, k):
        p = s * GROUP + k
        i = pairs[p, 0]
        j = pairs[p, 1]
        add = lambda total, term: term if total is None else total + term
        for chunk in range(chunks):
            for toward_first in (False, True):
                sums = [[None, None] for w in range(windows)]
                for c in range(part):
                    if toward_first:
                        at = pl.ds(k * rows + c, part, stride=part)
                    else:
                        at = pl.ds(k * rows + c * part, part)
                    g = out_re[s % 2, chunk, at]
                    h = out_im[s % 2, chunk, at]
                    for w in range(windows):
                        if toward_first:
                            a = row_of(j, w, 0, second_part, chunk, c)
                            b = row_of(j, w, 1, second_part, chunk, c)
                            re, im = g * a + h * b, g * b - h * a
                        else:
                            a = row_of(i, w, 0, first_part, chunk, c)
                            b = row_of(i, w, 1, first_part, chunk, c)
                            re, im = g * a - h * b, g * b + h * a
                        sums[w] = [add(sums[w][0], re), add(sums[w][1], im)]
                index = i if toward_first else j
                half = first_part if toward_first else second_part
                for w in range(windows):
                    for c in range(2):
                        grad[index, w, c, half, chunk] += sums[w][c]

    def start(s, fill):
        totals = [None] * GROUP
        edge = forward_edge(s)
        found = [forward(s, 0)]
        fill = list(fill)
        for call in fill[: len(fill) // 2]:
            call()
        shape_edge(s, edge, totals)
        for n in range(1, freq // wide):
            found.append(forward(s, n))
            shape(s, n - 1, found[n - 1], totals)
        for call in fill[len(fill) // 2 :]:
            call()
        shape(s, freq // wide - 1, found[-1], totals)
        tell(s, totals)

    for k in range(GROUP):
        cross(0, k)
    for copy in copies:
        copy.wait()
    start(0, [])
    for s in range(steps):
        fill = []
        late = []
        for k in range(GROUP):
            if s + 1 < steps:
                fill.append(functools.partial(cross, s + 1, k))
            if s > 0:
                (fill if k < GROUP // 2 or s + 1 == steps else late).append(
                    functools.partial(gradient, s - 1, k)
                )
        pieces = [(n, which) for n in range(freq // wide) for which in range(2)]
        share = -(-len(fill) // len(pieces))
        for m, (n, which) in enumerate(pieces):
            sums = back(s, n, which)
            for call in fill[m * share : (m + 1) * share]:
                call()
            scale_back(s, n, which, sums)
        if s + 1 < steps:
            start(s + 1, late)
    for k in range(GROUP):
        gradient(steps - 1, k)

    size = 2 * part
    for n in range(2 * count):
        index = meta[4 + n]
        target = keep if n < count else give
        for w in range(windows):
            m = mask[w, index].astype(jnp.float32)
            for c in range(2):
                at = (((n % count) * windows + w) * 2 + c) * size
                for chunk in range(chunks):
                    term = jnp.concatenate(
                        [grad[index, w, c, half, chunk] for half in range(2)], axis=0
                    )
                    to = slice(chunk * 128, (chunk + 1) * 128)
                    target[at : at + size, to] = (term * m).astype(target.dtype)
    give[count * windows * 2 * size :] = note_of(misfit[...], pair_count // 2)


def per_device(spectra, block_pairs, owners, window_mask):
    blk_count = lax.axis_size("blk")
    blk_index = lax.axis_index("blk")
    core = lax.axis_index("win")
    local = spectra.shape[0]
    channels = spectra.shape[3]
    freq = spectra.shape[4]
    part = channels // PARTS
    pair_total = block_pairs.shape[0]
    teams = blk_count // TEAM
    pair_count = pair_total // teams
    direct = teams == 1
    swap = [(0, 1), (1, 0)]
    smem = pl.BlockSpec(memory_space=pltpu.SMEM)
    vmem = pl.BlockSpec(memory_space=pltpu.VMEM)
    hbm = pl.BlockSpec(memory_space=pltpu.HBM)
    small = pltpu.CompilerParams(vmem_limit_bytes=SMALL_VMEM)
    count = len(HOPS[0])
    hop_pairs = [
        [(2 * b + c, 2 * (b ^ HOPS[c][r]) + c) for b in range(TEAM) for c in range(2)]
        for r in range(count)
    ]
    rank = blk_index if direct else lax.rem(blk_index, TEAM)
    meta = lax.dynamic_slice_in_dim(jnp.asarray(positions()), rank * 2 + core, 1)[0]
    if not direct:
        meta = meta.at[0].set(lax.div(blk_index, TEAM) * pair_count)

    owner_ids = owners[:, 0]
    order = jnp.arange(pair_total, dtype=jnp.int32)
    earlier = (owner_ids[:, None] == owner_ids[None, :]) & (order[None, :] < order[:, None])
    slot = owner_ids * CAP + jnp.sum(earlier.astype(jnp.int32), axis=1)
    mine_slots = blk_index * CAP + jnp.arange(CAP, dtype=jnp.int32)
    chosen = (slot[:, None] == mine_slots[None, :]).astype(jnp.float32)
    misfit_scale = 1.0 / (channels * channels * 2.0 * freq)

    if direct:
        other = lax.ppermute(spectra, "win", swap)
        parcel_type = jax.ShapeDtypeStruct((2 * local, 2, 2 * part, freq), jnp.bfloat16)
        parcels = pl.pallas_call(
            pack_kernel,
            out_shape=(parcel_type,) * count,
            in_specs=[smem, vmem, vmem],
            out_specs=(vmem,) * count,
            scratch_shapes=[pltpu.VMEM((PARTS, part, freq), jnp.float32)],
            compiler_params=small,
        )(meta, spectra, other)
        landed = [
            lax.ppermute(parcel, ("blk", "win"), pairs) for parcel, pairs in zip(parcels, hop_pairs)
        ]
        came = landed + [lax.ppermute(parcel, "win", swap) for parcel in landed]
    else:
        pieces = spectra[:, 0].reshape(local, 2, PARTS, part, freq)
        outgoing = jnp.stack(
            [jnp.stack([pieces[:, :, s] for s in SUBSETS[r]], axis=2) for r in range(TEAM)]
        ).reshape(TEAM, local, 2, 2 * part, freq)
        outgoing = jnp.tile(outgoing, (teams, 1, 1, 1, 1))
        own = lax.all_to_all(outgoing, "blk", split_axis=0, concat_axis=0, tiled=True)
        came = [own, lax.ppermute(own, "win", swap)]

    rows = part * part * GROUP
    parcel_rows = 2 * local * 2 * 2 * part
    misfit_type = jax.ShapeDtypeStruct((pair_count, 128), jnp.float32)
    if direct:
        split_shape = (blk_count, 2 * local, 2, 2, freq // 128, part, 128)
        keep, give, misfit = pl.pallas_call(
            team_kernel,
            out_shape=(
                jax.ShapeDtypeStruct((count * parcel_rows, freq), jnp.float32),
                jax.ShapeDtypeStruct((count * parcel_rows + pair_count // 2, freq), jnp.bfloat16),
                misfit_type,
            ),
            in_specs=[smem] * 3 + [vmem] * len(came) + [hbm] * 2 + [vmem] * 2,
            out_specs=(vmem, vmem, vmem),
            scratch_shapes=[
                pltpu.VMEM(split_shape, jnp.float32),
                pltpu.VMEM(split_shape, jnp.float32),
                pltpu.VMEM((2, rows, freq), jnp.bfloat16),
                pltpu.VMEM((2, rows, freq), jnp.bfloat16),
                pltpu.VMEM((2, rows, freq), jnp.bfloat16),
                pltpu.VMEM((2, rows, freq), jnp.bfloat16),
                pltpu.VMEM((2, rows, 128), jnp.float32),
                pltpu.VMEM((2, freq // 128, rows, 128), jnp.float32),
                pltpu.VMEM((2, freq // 128, rows, 128), jnp.float32),
                pltpu.VMEM((freq, freq), jnp.bfloat16),
                pltpu.VMEM((freq, freq), jnp.bfloat16),
                pltpu.SemaphoreType.DMA((2,)),
            ],
            compiler_params=pltpu.CompilerParams(vmem_limit_bytes=24 << 20),
        )(meta, block_pairs, window_mask, *came, *team_tables(freq))
        swapped = lax.ppermute(give, "win", swap)
        parcel_type = jax.ShapeDtypeStruct((parcel_rows + pair_count // 2, freq), jnp.bfloat16)
        parcels = pl.pallas_call(
            add_kernel,
            out_shape=(parcel_type,) * count,
            in_specs=[vmem] * 3,
            out_specs=(vmem,) * count,
            compiler_params=small,
        )(keep, swapped, misfit)
        landed = [
            lax.ppermute(parcel, ("blk", "win"), pairs) for parcel, pairs in zip(parcels, hop_pairs)
        ]
        landed += [lax.ppermute(parcel, "win", swap) for parcel in landed]
        gradient, totals = pl.pallas_call(
            functools.partial(merge_kernel, scale=misfit_scale),
            out_shape=(
                jax.ShapeDtypeStruct(spectra.shape, jnp.bfloat16),
                jax.ShapeDtypeStruct((1, CAP), jnp.float32),
            ),
            in_specs=[smem] + [vmem] * (len(landed) + 1),
            out_specs=(vmem, vmem),
            scratch_shapes=[pltpu.VMEM((local, 2, PARTS, part, freq), jnp.float32)],
            compiler_params=small,
        )(meta, *landed, chosen)
        return (gradient, totals.reshape(CAP))
    half = jax.ShapeDtypeStruct((blk_count, local, 2, 2 * part, freq), jnp.float32)
    own_grad, other_grad, misfit = pl.pallas_call(
        pair_kernel,
        out_shape=(half, half, jax.ShapeDtypeStruct((pair_count, freq), jnp.float32)),
        in_specs=[smem] * 3 + [vmem] * 7,
        out_specs=(vmem, vmem, vmem),
        scratch_shapes=[
            pltpu.VMEM((GROUP * 4 * local, part, freq), jnp.float32),
            pltpu.VMEM((GROUP * 4 * local, part, freq), jnp.float32),
            pltpu.VMEM((rows, freq), jnp.bfloat16),
            pltpu.VMEM((rows, freq), jnp.bfloat16),
            pltpu.VMEM((rows, 2 * freq), jnp.bfloat16),
            pltpu.VMEM((freq // 128, rows, 128), jnp.float32),
            pltpu.VMEM((freq // 128, rows, 128), jnp.float32),
        ],
        compiler_params=pltpu.CompilerParams(
            vmem_limit_bytes=(16 << 20) + 3 * math.prod(half.shape) * 4
        ),
    )(meta, block_pairs, window_mask, *came, *tables(freq))

    swapped = lax.ppermute(other_grad.astype(jnp.bfloat16), "win", swap)
    terms = jnp.sum(misfit, axis=1)
    terms = terms + lax.ppermute(terms, "win", swap)
    chip_grad = (own_grad + swapped.astype(jnp.float32)).astype(jnp.bfloat16)
    high = terms.astype(jnp.bfloat16)
    low = (terms - high.astype(jnp.float32)).astype(jnp.bfloat16)
    note = jnp.zeros((8, freq), jnp.bfloat16).at[0, :pair_count].set(high).at[1, :pair_count].set(low)
    grad_rows = local * 2 * 2 * part
    payload = jnp.concatenate(
        [
            chip_grad.reshape(blk_count, grad_rows, freq),
            jnp.broadcast_to(note[None], (blk_count, 8, freq)),
        ],
        axis=1,
    )
    arrived = lax.all_to_all(payload, "blk", split_axis=0, concat_axis=0, tiled=True)
    wide = arrived[:, :grad_rows].reshape(teams, TEAM, local, 2, 2, part, freq).astype(jnp.float32)
    wide = jnp.sum(wide, axis=0)
    gradient = jnp.stack(
        [
            sum(wide[r, :, :, SUBSETS[r].index(s)] for r in range(TEAM) if s in SUBSETS[r])
            for s in range(PARTS)
        ],
        axis=2,
    )
    gradient = gradient.reshape(local, 1, 2, channels, freq).astype(jnp.bfloat16)
    notes = arrived[:, grad_rows:, :pair_count].astype(jnp.float32)
    notes = jnp.sum((notes[:, 0] + notes[:, 1]).reshape(teams, TEAM, pair_count), axis=1)
    pair_misfit = notes.reshape(pair_total) * misfit_scale
    totals = jnp.sum(pair_misfit[:, None] * chosen, axis=0)
    return (gradient, totals)


def solution(mesh):
    return jax.shard_map(
        per_device,
        mesh=mesh,
        in_specs=(
            P("win", ("groups", "blk"), None, None, None),
            P("groups", None),
            P("groups", None),
            P(None, "groups"),
        ),
        out_specs=(P("win", ("groups", "blk"), None, None, None), P(("groups", "blk"))),
        check_vma=False,
    )
```
